512 devices in a mesh: inst: 64 (over z, y), head: 8 (over x, core).
Axes of the slice: x: 4, y: 4, z: 16, core: 2. Of those that a mesh axis runs over, the one named last changes fastest.
Arguments:
- prefill_codes: bfloat16 [2048, 64, 576], P('inst', 'head'), may hold values from -4 to 4
- prefill_scales: bfloat16 [2048, 64, 4], P('inst', 'head'), may hold values from 0.25 to 1
- page_lists: int32 [2048, 1], P('inst'), may hold values from 0 to 31, as said below
- req_lengths: int32 [2048], P('inst'), may hold values from 1 to 64
- destinations: int32 [2048], P('inst'), may hold values from 0 to 63, as said below
- pool_codes: bfloat16 [1024, 64, 576], P('inst'), may hold values from -4 to 4
- pool_scales: bfloat16 [1024, 64, 4], P('inst'), may hold values from 0.25 to 1
- res_tables: int32 [4096, 8], P('inst'), may hold values from 0 to 15, as said below
- res_lengths: int32 [4096], P('inst'), may hold values from 1 to 512
- queries: bfloat16 [2, 4096, 64, 576], P(None, 'inst', 'head'), may hold values from -48 to 48
- new_latents: bfloat16 [2, 4096, 576], P(None, 'inst'), may hold values from -6 to 6
- value_projection: bfloat16 [64, 512, 128], P('head'), may hold values from -0.75 to 0.75
Outputs:
- attn_out: bfloat16 [2, 4096, 8192], P(None, 'inst', 'head')
The draws below stay inside these ranges and needn't reach their ends.
Inputs may be any that keep to these rules, and one draw needn't show every extreme that they name: `page_lists`: the 32 requests of one owner list disjoint pages of its own pool, every page once. `destinations`: the 32 requests of one owner go to distinct decode groups; in every draw some group receives a request from every owner. `res_tables`: each row lists 8 distinct pages of its group's resident pages; different rows may list the same pages.
All inputs are finite; a program needn't handle non-finite values.
Results may differ from the reference program's by a relative error of at most 0.0068.
Values may be sent and summed in bfloat16 or wider, within the bound.
A program may use at most 192 MiB of HBM per device.

```python
import math
import jax
import jax.numpy as jnp
from jax import lax

LATENT_WIDTH = 512
TILE = 128
HEAD_COUNT = 64
VALUE_WIDTH = 128
PAGE = 64
PPR = 1
RP = 8
POOL = 16
ROWS = 64
LAT = 576
TILES = 4
REQ = 32
PREF_PAGES = 32
N_INST = 64


def latent_steps(key):
    first = jnp.clip(jax.random.normal(jax.random.fold_in(key, 11), (N_INST * ROWS, LAT), jnp.float32), -6.0, 6.0)
    second = jnp.clip(jax.random.normal(jax.random.fold_in(key, 12), (N_INST * ROWS, LAT), jnp.float32), -6.0, 6.0)
    row_ids = jnp.arange(N_INST * ROWS) % ROWS
    nearby = (row_ids < 8)[:, None]
    second = jnp.where(nearby, jnp.clip(second, -6.0, 6.0), second)
    return jnp.stack([first, second])


def permute_pages(owner_key):
    return jax.random.permutation(owner_key, REQ * PPR)


def permute_requests(owner_key):
    return jax.random.permutation(owner_key, REQ)


def permute_pool(row_key):
    return jax.random.permutation(row_key, POOL)[:RP]


def draw_page_lists(key, part):
    key = jax.random.fold_in(key, 1)
    orders = jax.vmap(permute_pages)(jax.random.split(key, N_INST))
    return orders.reshape(N_INST * REQ, PPR).astype(jnp.int32)


def draw_destinations(key, part):
    key = jax.random.fold_in(key, 2)
    hot_key, bias_key, score_key, order_key = jax.random.split(key, 4)
    hottest = jax.random.randint(hot_key, (), 0, N_INST)
    favour = jax.random.randint(bias_key, (N_INST,), 0, 4) * 262144
    noise = jax.random.randint(score_key, (N_INST, N_INST), 0, 262144)
    group_ids = jnp.arange(N_INST, dtype=jnp.int32)
    ranking = noise + favour[None, :] + jnp.where(group_ids == hottest, 2097152, 0)[None, :]
    ranking = ranking * N_INST + group_ids[None, :]
    chosen = lax.top_k(ranking, REQ)[1]
    shuffles = jax.vmap(permute_requests)(jax.random.split(order_key, N_INST))
    chosen = jnp.take_along_axis(chosen, shuffles, axis=1)
    return chosen.reshape(N_INST * REQ).astype(jnp.int32)


def draw_res_tables(key, part):
    key = jax.random.fold_in(key, 3)
    tables = jax.vmap(permute_pool)(jax.random.split(key, N_INST * ROWS))
    return tables.astype(jnp.int32)


def draw_new_latents(key, part):
    stepped = latent_steps(key)
    return stepped.astype(jnp.bfloat16)


def draw_queries(key, part):
    key = jax.random.fold_in(key, 5)
    full_shape = (2, N_INST * ROWS, HEAD_COUNT, LAT)
    drawn = jnp.clip(jax.random.normal(key, full_shape, jnp.float32), -6.0, 6.0)
    return drawn.astype(jnp.bfloat16)


def with_ends(result, key, least, top_value):
    longest = result.shape.index(max(result.shape))
    spots = []
    for shift in (0, 1):
        where = [jax.random.randint(jax.random.fold_in(key, axis), (), 0, length) for axis, length in enumerate(result.shape)]
        where[longest] = (where[longest] + shift) % result.shape[longest]
        spots.append(tuple(where))
    return result.at[spots[0]].set(least).at[spots[1]].set(top_value)


def shard_levels(rng, dims, pieces, smallest, high):
    level, own = 1.0, jax.random.fold_in(rng, 6)
    for axis_at, parts in pieces:
        draws = jnp.exp(jax.random.uniform(jax.random.fold_in(own, axis_at), (parts,), jnp.float32, smallest / len(pieces), high / len(pieces)))
        level = level * jnp.repeat(draws, dims[axis_at] // parts).reshape([-1 if axis == axis_at else 1 for axis in range(len(dims))])
    return level


def bell_draw(own_key, shape, deviation, limit, pieces=(), kind=jnp.bfloat16):
    result = jax.random.normal(own_key, shape, jnp.float32) * deviation
    if len(pieces) > 0:
        result = shard_levels(own_key, shape, pieces, -0.22, 0.18) * result
    return jnp.clip(result, min=-limit, max=limit).astype(kind)


def setup_inputs(seed: int = 0) -> dict:
    keys = jax.random.split(jax.random.key(seed), 13)
    prefill_codes = bell_draw(keys[0], (N_INST * PREF_PAGES, PAGE, LAT), 1.0, 4.0, ((0, 64), (1, 8)))
    prefill_scales = jnp.clip(jnp.exp(math.log(1.0) - 1.3862944 * jax.random.uniform(keys[1], (N_INST * PREF_PAGES, PAGE, TILES), jnp.float32) ** shard_levels(keys[1], (N_INST * PREF_PAGES, PAGE, TILES), ((0, 64), (1, 8)), -0.2, 0.2)), 0.25, 1.0).astype(jnp.bfloat16)
    page_lists = draw_page_lists(jax.random.fold_in(keys[12], 71), 0)
    req_lengths = with_ends(jax.random.randint(keys[3], (N_INST * REQ,), (PPR - 1) * PAGE + 1, PPR * PAGE + 1), jax.random.fold_in(keys[3], 1), (PPR - 1) * PAGE + 1, PPR * PAGE).astype(jnp.int32)
    destinations = draw_destinations(jax.random.fold_in(keys[12], 71), 0)
    pool_codes = bell_draw(keys[5], (N_INST * POOL, PAGE, LAT), 1.0, 4.0, ((0, 64),))
    pool_scales = jnp.clip(jnp.exp(math.log(1.0) - 1.3862944 * jax.random.uniform(keys[6], (N_INST * POOL, PAGE, TILES), jnp.float32) ** shard_levels(keys[6], (N_INST * POOL, PAGE, TILES), ((0, 64),), -0.2, 0.2)), 0.25, 1.0).astype(jnp.bfloat16)
    res_tables = draw_res_tables(jax.random.fold_in(keys[12], 71), 0)
    res_lengths = with_ends(jax.random.randint(keys[8], (N_INST * ROWS,), 1, RP * PAGE + 1), jax.random.fold_in(keys[8], 1), 1, RP * PAGE).astype(jnp.int32)
    queries = draw_queries(jax.random.fold_in(keys[12], 71), 0)
    new_latents = draw_new_latents(jax.random.fold_in(keys[12], 71), 0)
    value_projection = bell_draw(keys[11], (HEAD_COUNT, LATENT_WIDTH, VALUE_WIDTH), (LATENT_WIDTH // 8) ** -0.5, 0.75, ((0, 8),))
    return {"prefill_codes": prefill_codes, "prefill_scales": prefill_scales, "page_lists": page_lists, "req_lengths": req_lengths, "destinations": destinations, "pool_codes": pool_codes, "pool_scales": pool_scales, "res_tables": res_tables, "res_lengths": res_lengths, "queries": queries, "new_latents": new_latents, "value_projection": value_projection}


softmax_scale = (0.1 * math.log(40.0) + 1.0) ** 2 / math.sqrt(192.0)

def dequantize(decoded_values, tile_scales):
    spread_rows = jnp.repeat(tile_scales.astype(jnp.float32), TILE, axis=-1)
    latent_state = decoded_values[..., :LATENT_WIDTH].astype(jnp.float32) * spread_rows
    rotary_part = decoded_values[..., LATENT_WIDTH:].astype(jnp.float32)
    return jnp.concatenate([latent_state, rotary_part], axis=-1).astype(jnp.bfloat16)

def reference(prefill_codes, prefill_scales, page_lists, req_lengths, destinations, pool_codes, pool_scales, res_tables, res_lengths, queries, new_latents, value_projection):
    owner_dest = destinations.reshape(N_INST, REQ)
    owner_lists = page_lists.reshape(N_INST, REQ, PPR)
    owner_lengths = req_lengths.reshape(N_INST, REQ)
    owner_codes = prefill_codes.reshape(N_INST, PREF_PAGES, PAGE, LAT)
    owner_scales = prefill_scales.reshape(N_INST, PREF_PAGES, PAGE, TILES)
    group_codes = pool_codes.reshape(N_INST, POOL, PAGE, LAT)
    group_scales = pool_scales.reshape(N_INST, POOL, PAGE, TILES)
    group_tables = res_tables.reshape(N_INST, ROWS, RP)
    group_lengths = res_lengths.reshape(N_INST, ROWS)
    group_queries = queries.reshape(2, N_INST, ROWS, HEAD_COUNT, LAT)
    group_new = new_latents.reshape(2, N_INST, ROWS, LAT)
    owner_ids = jnp.arange(N_INST, dtype=jnp.int32)
    row_ids = jnp.arange(ROWS, dtype=jnp.int32)

    def one_group(group_index):
        matches = owner_dest == group_index
        present = jnp.any(matches, axis=1).astype(jnp.int32)
        chosen = lax.optimization_barrier(jnp.sum(matches.astype(jnp.int32) * jnp.arange(REQ, dtype=jnp.int32)[None, :], axis=1))
        slot_rank = jnp.cumsum(present) - 1
        arrivals = jnp.sum(present)
        picked = (present[None, :] == 1) & (slot_rank[None, :] == row_ids[:, None])
        owner_of_row = lax.optimization_barrier(jnp.sum(picked.astype(jnp.int32) * owner_ids[None, :], axis=1))
        arrived = row_ids < arrivals
        request = chosen[owner_of_row]
        page_ids = owner_lists[owner_of_row, request]
        arr_keys = dequantize(owner_codes[owner_of_row[:, None], page_ids], owner_scales[owner_of_row[:, None], page_ids])
        arr_keys = arr_keys.reshape(ROWS, PPR * PAGE, LAT)
        arr_len = jnp.where(arrived, owner_lengths[owner_of_row, request], 0)
        table_rows = group_tables[group_index]
        res_keys = dequantize(group_codes[group_index][table_rows], group_scales[group_index][table_rows])
        res_keys = res_keys.reshape(ROWS, RP * PAGE, LAT)
        res_len = jnp.where(arrived, 0, group_lengths[group_index])
        ctx_keys = jnp.concatenate([res_keys, arr_keys], axis=1)
        ctx_mask = jnp.concatenate([jnp.arange(RP * PAGE)[None, :] < res_len[:, None], jnp.arange(PPR * PAGE)[None, :] < arr_len[:, None]], axis=1)
        results = []
        for step_index in range(2):
            fresh_keys = jnp.moveaxis(group_new[:step_index + 1, group_index], 0, 1)
            combined_keys = jnp.concatenate([ctx_keys, fresh_keys], axis=1)
            key_mask = jnp.concatenate([ctx_mask, jnp.ones((ROWS, step_index + 1), dtype=bool)], axis=1)
            step_query = group_queries[step_index, group_index].astype(jnp.float32)
            scores = jnp.einsum('rhc,rkc->rhk', step_query, combined_keys.astype(jnp.float32)) * softmax_scale
            scores = jnp.where(key_mask[:, None, :], scores, -jnp.inf)
            highest = lax.optimization_barrier(jnp.max(scores, axis=-1, keepdims=True))
            weight_matrix = jnp.exp(scores - highest)
            weight_matrix = (weight_matrix / lax.optimization_barrier(jnp.sum(weight_matrix, axis=-1, keepdims=True))).astype(jnp.bfloat16)
            latent_state = jnp.einsum('luy,lyb->lub', weight_matrix.astype(jnp.float32), combined_keys[..., :LATENT_WIDTH].astype(jnp.float32)).astype(jnp.bfloat16)
            mixed_out = jnp.einsum('rhc,hcv->rhv', latent_state.astype(jnp.float32), value_projection.astype(jnp.float32)).astype(jnp.bfloat16)
            results.append(mixed_out.reshape(ROWS, HEAD_COUNT * VALUE_WIDTH))
        return jnp.stack(results)
    stacked = lax.map(one_group, owner_ids)
    return jnp.transpose(stacked, (1, 0, 2, 3)).reshape(2, N_INST * ROWS, HEAD_COUNT * VALUE_WIDTH)
```

```python
import math

import jax
import jax.numpy as jnp
from jax import lax
from jax.sharding import PartitionSpec as P

LATENT_WIDTH = 512
TILE = 128


softmax_scale = (0.1 * math.log(40.0) + 1.0) ** 2 / math.sqrt(192.0)
block_rows = 64


def dequantize(decoded_values, tile_scales):
    spread_rows = jnp.repeat(tile_scales.astype(jnp.float32), TILE, axis=-1)
    latent_state = decoded_values[..., :LATENT_WIDTH].astype(jnp.float32) * spread_rows
    rotary_part = decoded_values[..., LATENT_WIDTH:].astype(jnp.float32)
    return jnp.concatenate([latent_state, rotary_part], axis=-1).astype(jnp.bfloat16)


def to_blocks(array, axis):
    shape = array.shape
    blocks = shape[axis] // block_rows
    split = array.reshape(shape[:axis] + (blocks, block_rows) + shape[axis + 1 :])
    return jnp.moveaxis(split, axis, 0)


def shards(
    prefill_codes,
    prefill_scales,
    page_lists,
    req_lengths,
    destinations,
    pool_codes,
    pool_scales,
    res_tables,
    res_lengths,
    queries,
    new_latents,
    value_projection,
):
    group_count = lax.axis_size("inst")
    request_count = destinations.shape[0]
    row_count = res_tables.shape[0]
    page_size = pool_codes.shape[1]
    pool_pages = pool_codes.shape[0]
    table_width = res_tables.shape[1]
    width = pool_codes.shape[2]
    group_ids = jnp.arange(group_count, dtype=jnp.int32)
    matches = destinations[None, :] == group_ids[:, None]
    present = jnp.any(matches, axis=1)
    chosen = jnp.sum(
        matches.astype(jnp.int32) * jnp.arange(request_count, dtype=jnp.int32)[None, :], axis=1
    )
    slot_pages = page_lists[chosen]
    slot_lengths = jnp.where(present, req_lengths[chosen], 0)
    pool_keys = dequantize(pool_codes, pool_scales)
    flattened_pool = pool_keys.reshape(pool_pages * page_size, width)
    pref_keys = dequantize(prefill_codes, prefill_scales)
    recv_keys, recv_lengths = (
        lax.all_to_all(pref_keys[slot_pages[:, 0]], "inst", split_axis=0, concat_axis=0, tiled=True),
        lax.all_to_all(slot_lengths, "inst", split_axis=0, concat_axis=0, tiled=True),
    )
    recv_keys = lax.all_gather(recv_keys, "head", axis=1, tiled=True)
    present_src = (recv_lengths > 0).astype(jnp.int32)
    slot_rank = jnp.cumsum(present_src) - 1
    arrivals = jnp.sum(present_src)
    row_ids = jnp.arange(row_count, dtype=jnp.int32)
    picked = (present_src[None, :] == 1) & (slot_rank[None, :] == row_ids[:, None])
    anchor = jnp.sum(picked.astype(jnp.int32) * group_ids[None, :], axis=1)
    arrived = row_ids < arrivals
    arr_len = jnp.where(arrived, recv_lengths[anchor], 0)
    arr_keys = recv_keys[anchor]
    arr_mask = jnp.arange(arr_keys.shape[1], dtype=jnp.int32)[None, :] < arr_len[:, None]
    table_hit = res_tables[:, :, None] == jnp.arange(pool_pages, dtype=jnp.int32)[None, None, :]
    listed = jnp.any(table_hit, axis=1)
    start_pos = jnp.sum(
        table_hit.astype(jnp.int32)
        * (jnp.arange(table_width, dtype=jnp.int32) * page_size)[None, :, None],
        axis=1,
    )
    token_pos = start_pos[:, :, None] + jnp.arange(page_size, dtype=jnp.int32)[None, None, :]
    res_valid = (listed[:, :, None] & (token_pos < res_lengths[:, None, None])).reshape(
        row_count, pool_pages * page_size
    )
    res_extra = (res_valid & jnp.logical_not(arrived)[:, None],)

    def run_block(parts):
        query_pair, new_pair, block_arriving, block_arr_mask, extra = parts
        res_mask = extra[0]
        score_form = "rhc,kc->rhk"
        mix_form = "rhk,kc->rhc"
        resident_latent = flattened_pool[..., :LATENT_WIDTH]
        arriving_latent = block_arriving[..., :LATENT_WIDTH]
        outputs = []
        for step_index in range(2):
            step_query = query_pair[step_index]
            fresh_keys = jnp.moveaxis(new_pair[: step_index + 1], 0, 1)
            res_scores = (
                jnp.einsum(
                    score_form, step_query, flattened_pool, preferred_element_type=jnp.float32
                )
                * softmax_scale
            )
            arr_scores = (
                jnp.einsum(
                    "rhc,rkc->rhk", step_query, block_arriving, preferred_element_type=jnp.float32
                )
                * softmax_scale
            )
            new_scores = (
                jnp.einsum(
                    "rhc,rjc->rhj", step_query, fresh_keys, preferred_element_type=jnp.float32
                )
                * softmax_scale
            )
            res_scores = jnp.where(res_mask[:, None, :], res_scores, -jnp.inf)
            arr_scores = jnp.where(block_arr_mask[:, None, :], arr_scores, -jnp.inf)
            highest = jnp.maximum(
                jnp.maximum(
                    jnp.max(res_scores, axis=-1, keepdims=True),
                    jnp.max(arr_scores, axis=-1, keepdims=True),
                ),
                jnp.max(new_scores, axis=-1, keepdims=True),
            )
            res_exp = jnp.exp(res_scores - highest)
            arr_exp = jnp.exp(arr_scores - highest)
            new_exp = jnp.exp(new_scores - highest)
            denominator = (
                jnp.sum(res_exp, axis=-1, keepdims=True)
                + jnp.sum(arr_exp, axis=-1, keepdims=True)
                + jnp.sum(new_exp, axis=-1, keepdims=True)
            )
            res_weights = (res_exp / denominator).astype(jnp.bfloat16)
            arr_weights = (arr_exp / denominator).astype(jnp.bfloat16)
            new_weights = (new_exp / denominator).astype(jnp.bfloat16)
            latent_state = jnp.einsum(
                mix_form, res_weights, resident_latent, preferred_element_type=jnp.float32
            )
            latent_state = latent_state + jnp.einsum(
                "luy,lyb->lub", arr_weights, arriving_latent, preferred_element_type=jnp.float32
            )
            latent_state = latent_state + jnp.einsum(
                "rhj,rjc->rhc",
                new_weights,
                fresh_keys[..., :LATENT_WIDTH],
                preferred_element_type=jnp.float32,
            )
            latent_state = latent_state.astype(jnp.bfloat16)
            mixed_out = jnp.einsum(
                "rhc,hcv->rhv", latent_state, value_projection, preferred_element_type=jnp.float32
            ).astype(jnp.bfloat16)
            outputs.append(mixed_out.reshape(mixed_out.shape[0], -1))
        return jnp.stack(outputs)

    block_extra = tuple((to_blocks(item, 0) for item in res_extra))
    inputs = (
        to_blocks(queries, 1),
        to_blocks(new_latents, 1),
        to_blocks(arr_keys, 0),
        to_blocks(arr_mask, 0),
        block_extra,
    )
    stacked = lax.map(run_block, inputs)
    stacked = jnp.moveaxis(stacked, 0, 1)
    return stacked.reshape(2, row_count, stacked.shape[-1])


def solution(mesh):
    return jax.shard_map(
        shards,
        mesh=mesh,
        in_specs=(
            P("inst", "head", None),
            P("inst", "head", None),
            P("inst", None),
            P("inst"),
            P("inst"),
            P("inst", None, None),
            P("inst", None, None),
            P("inst", None),
            P("inst"),
            P(None, "inst", "head", None),
            P(None, "inst", None),
            P("head", None, None),
        ),
        out_specs=P(None, "inst", "head"),
        check_vma=False,
    )
```

```python
import functools
import math

import jax
import jax.numpy as jnp
from jax import lax
from jax.experimental import pallas as pl
from jax.experimental.pallas import tpu as pltpu
from jax.sharding import PartitionSpec as P

LATENT_WIDTH = 512
LAT = 576
WIDE = 640
NZ, NY, NX = 16, 4, 4
SLOTS = NZ * NY // 2
CHUNKS = SLOTS // 4
BIG = 1e30
MESH = pl.DeviceIdType.MESH
softmax_scale = (0.1 * math.log(40.0) + 1.0) ** 2 / math.sqrt(192.0)
F32, BF16, I32 = jnp.float32, jnp.bfloat16, jnp.int32


def iota(shape, axis):
    return lax.broadcasted_iota(I32, shape, axis)


def dot(a, b):
    return lax.dot_general(a, b, (((1,), (0,)), ((), ())), preferred_element_type=F32)


def dot_t(a, b):
    return lax.dot_general(a, b, (((1,), (1,)), ((), ())), preferred_element_type=F32)


def slot_offset(m, core):
    q, sign, half = m // 4, (m // 2) % 2, m % 2
    if isinstance(m, int):
        dz = q if sign == 0 else (NZ - q if q else NZ // 2)
    else:
        dz = jnp.where(sign == 0, q, jnp.where(q == 0, NZ // 2, NZ - q))
    return dz, 2 * half + core


def dequantize_into(dst, codes, scales, rows, start):
    for tile in range(4):
        lanes = slice(tile * 128, tile * 128 + 128)
        dst[start : start + rows, lanes] = (
            codes[:, lanes].astype(F32) * scales[:, tile : tile + 1].astype(F32)
        ).astype(BF16)
    dst[start : start + rows, 512:LAT] = codes[:, 512:LAT]


def softmax_mix(scores, fresh_scores, values, fresh_values):
    scores = scores * softmax_scale
    fresh_scores = fresh_scores * softmax_scale
    highest = jnp.maximum(
        jnp.max(scores, axis=1, keepdims=True), jnp.max(fresh_scores, axis=1, keepdims=True)
    )
    weights = jnp.exp(scores - highest)
    fresh_weights = jnp.exp(fresh_scores - highest)
    total = jnp.sum(weights, axis=1, keepdims=True) + jnp.sum(fresh_weights, axis=1, keepdims=True)
    mixed = dot(weights.astype(BF16), values) + dot(fresh_weights.astype(BF16), fresh_values)
    return (mixed / total).astype(BF16)


def kernel(
    codes, scales, pages, lengths, dests, pool_codes, pool_scales, tables, res_lengths,
    queries, fresh, projection, out,
    keys, packed, pages_in, res_keys, wide_q, slot_q, slot_fresh, slot_lat, lat,
    key_send, key_recv, a_send, a_recv, r_send, r_recv, l_send, l_recv,
    rr_send, rr_recv, ll_send, ll_recv, p_send, p_recv, own_sem,
):
    inst, head = lax.axis_index("inst"), lax.axis_index("head")
    z, y = inst // NY, inst % NY
    x, core = head // 2, head % 2
    right_x, left_x, far_x = (x + 1) % NX, (x + NX - 1) % NX, (x + 2) % NX
    right, left = (inst, right_x * 2 + core), (inst, left_x * 2 + core)
    partner = (inst, x * 2 + 1 - core)

    def target(m):
        dz, dy = slot_offset(m, core)
        return (((z + dz) % NZ) * NY + (y + dy) % NY, head)

    barrier = pltpu.get_barrier_semaphore()
    for device in (partner, right, left):
        pl.semaphore_signal(barrier, inc=1, device_id=device, device_id_type=MESH)
    for m in range(SLOTS):
        if m == 0:
            @pl.when(core == 1)
            def _():
                pl.semaphore_signal(barrier, inc=1, device_id=target(0), device_id_type=MESH)
        else:
            pl.semaphore_signal(barrier, inc=1, device_id=target(m), device_id_type=MESH)

    own = keys.at[core]
    own[:, 512:WIDE] = jnp.zeros((256, 128), BF16)
    dequantize_into(own, codes, scales, 256, 0)

    pl.semaphore_wait(barrier, SLOTS + 2 + core)
    key_copy = pltpu.make_async_remote_copy(
        src_ref=own, dst_ref=own, send_sem=key_send, recv_sem=key_recv,
        device_id=partner, device_id_type=MESH,
    )
    key_copy.start()

    rows = SLOTS * 16
    row = iota((rows, 32), 0)
    dz, dy = slot_offset(row // 16, core)
    wanted = ((z + dz) % NZ) * NY + (y + dy) % NY
    hit = dests[...] == wanted
    page = jnp.sum(jnp.where(hit, pages[...].astype(F32) + 1.0, 0.0), axis=1, keepdims=True)
    count = jnp.sum(jnp.where(hit, lengths[...].astype(F32), 0.0), axis=1, keepdims=True)
    slot_row = iota((rows, 1), 0)
    token = slot_row % 16
    column = (token // 8) * 256 + (page.astype(I32) - 1) * 8 + token % 8
    column = jnp.where(page > 0.5, column, -1)
    choose = jnp.where(column == iota((rows, 512), 1), 1.0, 0.0).astype(BF16)
    valid = (x * 16 + token).astype(F32) < count
    lane = iota((rows, 128), 1)
    mine = (lane - 64) == (slot_row // 16) % 4
    bias = jnp.where(lane < 68, jnp.where(mine & valid, 0.0, -BIG), 0.0)

    key_copy.wait()
    both = keys[...].reshape(512, WIDE)
    for tile in range(4):
        lanes = slice(tile * 128, tile * 128 + 128)
        packed[:, :, lanes] = dot(choose, both[:, lanes]).astype(BF16).reshape(SLOTS, 16, 128)
    last = dot(choose, both[:, 512:WIDE])
    packed[:, :, 512:WIDE] = jnp.where(lane < 64, last, bias).astype(BF16).reshape(SLOTS, 16, 128)

    def a_copy(m):
        return pltpu.make_async_remote_copy(
            src_ref=packed.at[m], dst_ref=pages_in.at[core, m // 4, x, m % 4],
            send_sem=a_send.at[m], recv_sem=a_recv.at[m],
            device_id=target(m), device_id_type=MESH,
        )

    own_copy = pltpu.make_async_copy(packed.at[0], pages_in.at[core, 0, x, 0], own_sem)
    order = list(range(1, CHUNKS)) + [0]
    for q in order:
        for m in range(4 * q, 4 * q + 4):
            if m == 0:
                pl.when(core == 1)(lambda: a_copy(0).start())
                pl.when(core == 0)(lambda: own_copy.start())
            else:
                a_copy(m).start()

    def resident_keys():
        listed = jnp.zeros((128, 16), F32)
        page_ids = iota((64, 16), 1)
        for j in range(8):
            left_over = jnp.clip(res_lengths[...].astype(F32) - 64.0 * j, 0.0, 64.0)
            part = jnp.where(tables[:, j : j + 1] == page_ids, left_over, 0.0)
            listed = listed + jnp.concatenate([part, part], axis=0)
        spread = jnp.where(iota((1024, 16), 0) // 64 == iota((1024, 16), 1), 1.0, 0.0).astype(BF16)
        held = dot_t(spread, listed.astype(BF16))
        place = (iota((1024, 128), 0) % 64).astype(F32)
        res_keys[0:1024, 512:WIDE] = jnp.where(place < held, 0.0, -BIG).astype(BF16)
        dequantize_into(res_keys, pool_codes, pool_scales, 1024, 0)
        same = iota((128, 128), 0) % 64 == iota((128, 128), 1) - 64
        res_keys[1024:1152, 512:WIDE] = jnp.where(same, 0.0, -BIG).astype(BF16)
        res_keys[1024:1152, 0:LAT] = fresh[...]
        row_of = (iota((1024, 128), 0) // 8) % 64
        wide_q[:, 512:WIDE] = jnp.where(row_of == iota((1024, 128), 1) - 64, 1.0, 0.0).astype(BF16)
        wide_q[:, 0:LAT] = queries[...]

    def resident_block(block):
        rows_at = slice(block * 128, block * 128 + 128)
        query = wide_q[rows_at, :]
        scores = dot_t(query, res_keys[0:1024, :])
        fresh_scores = dot_t(query, res_keys[1024:1152, :])
        if block < 4:
            fresh_scores = jnp.where(iota((128, 128), 1) < 64, fresh_scores, -BIG)
        mixed = softmax_mix(
            scores, fresh_scores, res_keys[0:1024, 0:512], res_keys[1024:1152, 0:512]
        ).astype(F32)
        for tile in range(4):
            lat[tile, rows_at, :] = mixed[:, tile * 128 : tile * 128 + 128]

    def hop(src_x, piece, q, sems, device):
        send, recv = sems
        ref = pages_in.at[core, q, src_x, piece]
        return pltpu.make_async_remote_copy(
            src_ref=ref, dst_ref=ref, send_sem=send.at[q], recv_sem=recv.at[q],
            device_id=device, device_id_type=MESH,
        )

    def to_partner(src_x, q, which, from_core):
        ref = pages_in.at[from_core, q, src_x]
        return pltpu.make_async_remote_copy(
            src_ref=ref, dst_ref=ref, send_sem=p_send.at[q, which], recv_sem=p_recv.at[q, which],
            device_id=partner, device_id_type=MESH,
        )

    whole, first, second = pl.ds(0, 4), pl.ds(0, 2), pl.ds(2, 2)
    right_sems, left_sems = (r_send, r_recv), (l_send, l_recv)
    far_right, far_left = (rr_send, rr_recv), (ll_send, ll_recv)

    def stage_own(q):
        for m in range(4 * q, 4 * q + 4):
            if m == 0:
                pl.when(core == 1)(lambda: a_copy(0).wait_recv())
                pl.when(core == 0)(lambda: own_copy.wait())
            else:
                a_copy(m).wait_recv()
        hop(x, whole, q, right_sems, right).start()
        hop(x, whole, q, left_sems, left).start()
        to_partner(x, q, 0, core).start()

    def stage_near(q):
        hop(left_x, whole, q, right_sems, right).wait_recv()
        hop(left_x, first, q, far_right, right).start()
        to_partner(left_x, q, 1, core).start()
        hop(right_x, whole, q, left_sems, left).wait_recv()
        hop(right_x, second, q, far_left, left).start()
        to_partner(right_x, q, 2, core).start()

    def stage_far(q):
        hop(far_x, first, q, far_right, right).wait_recv()
        hop(far_x, second, q, far_left, left).wait_recv()
        to_partner(far_x, q, 3, core).start()

    def stage_done(q):
        for which, src_x in enumerate((x, left_x, right_x, far_x)):
            to_partner(src_x, q, which, 1 - core).wait_recv()

    resident_keys()
    for step in range(CHUNKS + 3):
        if step < 8:
            resident_block(step)
        if step < CHUNKS:
            stage_own(order[step])
        if 1 <= step < CHUNKS + 1:
            stage_near(order[step - 1])
        if 2 <= step < CHUNKS + 2:
            stage_far(order[step - 2])
        if 3 <= step:
            stage_done(order[step - 3])

    slots = 2 * SLOTS
    tail = pages_in[:, :, 0, :, :, 512:WIDE].reshape(slots * 16, 128)
    heads_of = jnp.where(iota((slots, slots * 16), 1) == iota((slots, slots * 16), 0) * 16, 1.0, 0.0)
    marks = dot(heads_of.astype(BF16), tail)
    k_of = iota((slots, 128), 0)
    marks = jnp.where(iota((slots, 128), 1) == 64 + k_of % 4, marks, -BIG)
    present = jnp.where(jnp.max(marks, axis=1, keepdims=True) > -1.0, 1.0, 0.0)

    def owner_of(k):
        dz, dy = slot_offset(k % SLOTS, k // SLOTS)
        return ((z + NZ - dz) % NZ) * NY + (y + 2 * NY - dy) % NY

    eye = iota((slots, slots), 0) == iota((slots, slots), 1)
    present_row = dot(jnp.ones((slots, slots), BF16), jnp.where(eye, present, 0.0).astype(BF16))
    before = owner_of(iota((slots, slots), 1)) < owner_of(iota((slots, slots), 0))
    rank = jnp.sum(jnp.where(before, present_row, 0.0), axis=1, keepdims=True)
    arrivals = jnp.sum(present_row[0:8, :], axis=1, keepdims=True)[0:1, :]
    rank = jnp.where(present > 0.5, rank, -1.0)
    slot_rows = slots * 8
    widen = jnp.where(iota((slot_rows, slots), 0) // 8 == iota((slot_rows, slots), 1), 1.0, 0.0)
    rank_col = dot(widen.astype(BF16), jnp.broadcast_to(rank, (slots, 128)).astype(BF16))[:, 0:1]
    head_col = (iota((slot_rows, 1), 0) % 8).astype(F32)
    goal_col = jnp.where(rank_col > -0.5, rank_col * 8.0 + head_col, -1.0).astype(I32)
    to_slots = jnp.where(goal_col == iota((slot_rows, 512), 1), 1.0, 0.0).astype(BF16)
    narrow = jnp.where(iota((slots, slot_rows), 1) // 8 == iota((slots, slot_rows), 0), rank, 0.0)
    rank_row = dot(jnp.ones((8, slots), BF16), narrow.astype(BF16))[0:1, :]
    head_row = (iota((1, slot_rows), 1) % 8).astype(F32)
    goal_row = jnp.where(rank_row > -0.5, rank_row * 8.0 + head_row, -1.0).astype(I32)
    to_rows = jnp.where(goal_row == iota((512, slot_rows), 0), 1.0, 0.0).astype(BF16)
    fresh_pick = jnp.where(rank.astype(I32) == iota((slots, 64), 1), 1.0, 0.0).astype(BF16)
    slot_fresh[:, 512:WIDE] = jnp.zeros((2 * slots, 128), BF16)
    for j in range(2):
        slot_fresh[j * slots : (j + 1) * slots, 0:LAT] = dot(
            fresh_pick, fresh[j * 64 : j * 64 + 64, :]
        ).astype(BF16)
    for s in range(2):
        at = slice(s * slot_rows, (s + 1) * slot_rows)
        got = dot(to_slots, wide_q[s * 512 : s * 512 + 512, :])
        slot_q[at, 0:512] = got[:, 0:512].astype(BF16)
        lane = iota((slot_rows, 128), 1)
        mark = jnp.where(lane - 64 == (iota((slot_rows, 128), 0) // 8) % 4, 1.0, 0.0)
        slot_q[at, 512:WIDE] = jnp.where(lane < 64, got[:, 512:WIDE], mark).astype(BF16)

    def arrived_block(block):
        page_keys = pages_in[block // CHUNKS, block % CHUNKS].reshape(256, WIDE)
        query = jnp.concatenate(
            [
                slot_q[block * 32 : block * 32 + 32, :],
                slot_q[slot_rows + block * 32 : slot_rows + block * 32 + 32, :],
            ],
            axis=0,
        )
        scores = dot_t(query, page_keys)
        fresh_scores = dot_t(query, slot_fresh[...])
        row = iota((64, 2 * slots), 0)
        lane = iota((64, 2 * slots), 1)
        step = row // 32
        slot = block * 4 + (row % 32) // 8
        fresh_ok = (lane % slots == slot) & (lane // slots <= step)
        fresh_scores = jnp.where(fresh_ok, fresh_scores, -BIG)
        mixed = softmax_mix(scores, fresh_scores, page_keys[:, 0:512], slot_fresh[:, 0:512])
        slot_lat[block * 32 : block * 32 + 32, :] = mixed[0:32]
        slot_lat[slot_rows + block * 32 : slot_rows + block * 32 + 32, :] = mixed[32:64]

    for block in range(2 * CHUNKS):
        arrived_block(block)

    resident_row = (iota((512, 1), 0) // 8).astype(F32) >= arrivals
    for s in range(2):
        rows_at = slice(s * 512, s * 512 + 512)
        moved = dot(to_rows, slot_lat[s * slot_rows : (s + 1) * slot_rows, :])
        for tile in range(4):
            part = moved[:, tile * 128 : tile * 128 + 128]
            lat[tile, rows_at, :] = jnp.where(resident_row, lat[tile, rows_at, :], part)
    for h in range(8):
        per_head = jnp.concatenate(
            [lat[tile, pl.ds(h, 128, stride=8), :].astype(BF16) for tile in range(4)], axis=1
        )
        out[:, h * 128 : h * 128 + 128] = dot(per_head, projection[h]).astype(BF16)

    key_copies = [
        (hop(x, whole, q, right_sems, right), hop(x, whole, q, left_sems, left),
         hop(left_x, first, q, far_right, right), hop(right_x, second, q, far_left, left))
        for q in range(CHUNKS)
    ]
    for q in range(CHUNKS):
        for copy in key_copies[q]:
            copy.wait_send()
        for which, src_x in enumerate((x, left_x, right_x, far_x)):
            to_partner(src_x, q, which, core).wait_send()
    pl.when(core == 1)(lambda: a_copy(0).wait_send())
    for m in range(1, SLOTS):
        a_copy(m).wait_send()


def shards(
    prefill_codes, prefill_scales, page_lists, req_lengths, destinations, pool_codes, pool_scales,
    res_tables, res_lengths, queries, new_latents, value_projection,
):
    slots = 2 * SLOTS
    dma = pltpu.SemaphoreType.DMA
    result = pl.pallas_call(
        kernel,
        out_shape=jax.ShapeDtypeStruct((128, 1024), BF16),
        in_specs=[pl.BlockSpec(memory_space=pltpu.VMEM)] * 12,
        out_specs=pl.BlockSpec(memory_space=pltpu.VMEM),
        scratch_shapes=[
            pltpu.VMEM((2, 256, WIDE), BF16),
            pltpu.VMEM((SLOTS, 16, WIDE), BF16),
            pltpu.VMEM((2, CHUNKS, NX, 4, 16, WIDE), BF16),
            pltpu.VMEM((1152, WIDE), BF16),
            pltpu.VMEM((1024, WIDE), BF16),
            pltpu.VMEM((2 * slots * 8, WIDE), BF16),
            pltpu.VMEM((2 * slots, WIDE), BF16),
            pltpu.VMEM((2 * slots * 8, 512), BF16),
            pltpu.VMEM((4, 1024, 128), F32),
            dma, dma, dma((SLOTS,)), dma((SLOTS,)),
            dma((CHUNKS,)), dma((CHUNKS,)), dma((CHUNKS,)), dma((CHUNKS,)),
            dma((CHUNKS,)), dma((CHUNKS,)), dma((CHUNKS,)), dma((CHUNKS,)),
            dma((CHUNKS, 4)), dma((CHUNKS, 4)), dma,
        ],
        compiler_params=pltpu.CompilerParams(
            collective_id=0, has_side_effects=True, vmem_limit_bytes=48 * 1024 * 1024
        ),
    )(
        prefill_codes.reshape(256, LAT),
        prefill_scales.reshape(256, 4),
        page_lists.reshape(1, 32),
        req_lengths.reshape(1, 32),
        destinations.reshape(1, 32),
        pool_codes.reshape(1024, LAT),
        pool_scales.reshape(1024, 4),
        res_tables,
        res_lengths.reshape(64, 1),
        queries.reshape(1024, LAT),
        new_latents.reshape(128, LAT),
        value_projection,
    )
    return result.reshape(2, 64, 1024)


def solution(mesh):
    return jax.shard_map(
        shards,
        mesh=mesh,
        in_specs=(
            P("inst", "head", None),
            P("inst", "head", None),
            P("inst", None),
            P("inst"),
            P("inst"),
            P("inst", None, None),
            P("inst", None, None),
            P("inst", None),
            P("inst"),
            P(None, "inst", "head", None),
            P(None, "inst", None),
            P("head", None, None),
        ),
        out_specs=P(None, "inst", "head"),
        check_vma=False,
    )
```

```python
import functools
import math

import jax
import jax.numpy as jnp
from jax import lax
from jax.experimental import pallas as pl
from jax.experimental.pallas import tpu as pltpu
from jax.sharding import PartitionSpec as P

LATENT_WIDTH = 512
LAT = 576
WIDE = 640
NZ, NY, NX = 16, 4, 4
SLOTS = NZ * NY // 2
BLOCKS = 2 * SLOTS // 4
GROUPS = ((0, 6), (6, 10), (10, 14), (14, 18), (18, 22), (22, 26), (26, 30), (30, 32))
LAST = len(GROUPS) - 1
BIG = 1e30
MESH = pl.DeviceIdType.MESH
softmax_scale = (0.1 * math.log(40.0) + 1.0) ** 2 / math.sqrt(192.0)
F32, BF16, I32 = jnp.float32, jnp.bfloat16, jnp.int32


def iota(shape, axis):
    return lax.broadcasted_iota(I32, shape, axis)


def dot(a, b):
    return lax.dot_general(a, b, (((1,), (0,)), ((), ())), preferred_element_type=F32)


def dot_t(a, b):
    return lax.dot_general(a, b, (((1,), (1,)), ((), ())), preferred_element_type=F32)


def slot_offset(m, core):
    pair = m // 2
    if isinstance(m, int):
        dz = (pair + 1) // 2 if pair % 2 else (NZ - pair // 2) % NZ
    else:
        dz = jnp.where(pair % 2 == 1, (pair + 1) // 2, (NZ - pair // 2) % NZ)
    return dz, 2 * (m % 2) + core


def spread_scales(scales):
    n = scales.shape[1]
    scales = scales.astype(F32)
    spread = [jnp.broadcast_to(scales[j : j + 1, :], (128, n)) for j in range(4)]
    return jnp.concatenate(spread, axis=0).astype(BF16)


def softmax_mix(scores, fresh_scores, values, fresh_values):
    scores = scores * softmax_scale
    fresh_scores = fresh_scores * softmax_scale
    highest = jnp.maximum(
        jnp.max(scores, axis=1, keepdims=True), jnp.max(fresh_scores, axis=1, keepdims=True)
    )
    weights = jnp.exp(scores - highest)
    fresh_weights = jnp.exp(fresh_scores - highest)
    total = jnp.sum(weights, axis=1, keepdims=True) + jnp.sum(fresh_weights, axis=1, keepdims=True)
    mixed = dot(weights.astype(BF16), values) + dot(fresh_weights.astype(BF16), fresh_values)
    return (mixed / total).astype(BF16)


def kernel(
    codes_hbm, scales_hbm, pages_hbm, lengths_hbm, dests_hbm, pool_codes_hbm, pool_scales_hbm,
    tables_hbm, res_lengths_hbm, queries_hbm, fresh_hbm, projection_hbm, out,
    codes, scales, pages, lengths, dests, pool_codes, pool_scales,
    tables, res_lengths, queries, fresh, projection,
    keys, packed, pages_in, res_keys, wide_q, slot_q, slot_fresh, slot_lat, lat,
    in_sems, key_send, key_recv, a_send, a_recv, r_send, r_recv, l_send, l_recv,
    rr_send, rr_recv, ll_send, ll_recv, p_send, p_recv, own_sem,
):
    sources = (
        codes_hbm, scales_hbm, pages_hbm, lengths_hbm, dests_hbm, pool_codes_hbm, pool_scales_hbm,
        tables_hbm, res_lengths_hbm, queries_hbm, fresh_hbm, projection_hbm,
    )
    places = (
        codes, scales, pages, lengths, dests, pool_codes, pool_scales,
        tables, res_lengths, queries, fresh, projection,
    )
    fetches = [
        pltpu.make_async_copy(src, dst, in_sems.at[i])
        for i, (src, dst) in enumerate(zip(sources, places))
    ]
    for i in range(5):
        fetches[i].start()
    inst, head = lax.axis_index("inst"), lax.axis_index("head")
    z, y = inst // NY, inst % NY
    x, core = head // 2, head % 2
    right_x, left_x, far_x = (x + 1) % NX, (x + NX - 1) % NX, (x + 2) % NX
    right, left, far = (inst, right_x * 2 + core), (inst, left_x * 2 + core), (inst, far_x * 2 + core)
    partner = (inst, x * 2 + 1 - core)

    def target(m):
        dz, dy = slot_offset(m, core)
        return (((z + dz) % NZ) * NY + (y + dy) % NY, head)

    barrier = pltpu.get_barrier_semaphore()
    for device in (partner, right, left, far):
        pl.semaphore_signal(barrier, inc=1, device_id=device, device_id_type=MESH)
    for m in range(SLOTS):
        if m == 0:
            @pl.when(core == 1)
            def _():
                pl.semaphore_signal(barrier, inc=1, device_id=target(0), device_id_type=MESH)
        else:
            pl.semaphore_signal(barrier, inc=1, device_id=target(m), device_id_type=MESH)

    for i in range(5, len(fetches)):
        fetches[i].start()

    own = keys.at[core]
    own[:, 512:WIDE] = jnp.zeros((256, 128), BF16)
    fetches[0].wait()
    fetches[1].wait()
    token_row = iota((256, 32), 0)
    of_page = token_row // 8 == iota((256, 32), 1)
    scale_map = jnp.zeros((256, 512), F32)
    for t in range(8):
        at_token = jnp.where(of_page & (token_row % 8 == t), 1.0, 0.0).astype(BF16)
        scale_map = scale_map + dot_t(at_token, spread_scales(scales[t]))
    own[:, 0:512] = (codes[:, 0:512].astype(F32) * scale_map).astype(BF16)
    own[:, 512:LAT] = codes[:, 512:LAT]
    for i in range(2, 5):
        fetches[i].wait()

    pl.semaphore_wait(barrier, SLOTS + 3 + core)
    key_copy = pltpu.make_async_remote_copy(
        src_ref=own, dst_ref=own, send_sem=key_send, recv_sem=key_recv,
        device_id=partner, device_id_type=MESH,
    )
    key_copy.start()

    rows = SLOTS * 16
    row = iota((rows, 32), 0)
    dz, dy = slot_offset(row // 16, core)
    wanted = ((z + dz) % NZ) * NY + (y + dy) % NY
    hit = dests[...] == wanted
    page = jnp.sum(jnp.where(hit, pages[...].astype(F32) + 1.0, 0.0), axis=1, keepdims=True)
    count = jnp.sum(jnp.where(hit, lengths[...].astype(F32), 0.0), axis=1, keepdims=True)
    slot_row = iota((rows, 1), 0)
    token = slot_row % 16
    column = (token // 8) * 256 + (page.astype(I32) - 1) * 8 + token % 8
    column = jnp.where(page > 0.5, column, -1)
    choose = jnp.where(column == iota((rows, 512), 1), 1.0, 0.0).astype(BF16)
    valid = (x * 16 + token).astype(F32) < count
    lane = iota((rows, 128), 1)
    mine = (lane - 64) == (slot_row // 16) % 4
    bias = jnp.where(lane < 68, jnp.where(mine & valid, 0.0, -BIG), 0.0)

    key_copy.wait()
    both = keys[...].reshape(512, WIDE)
    for tile in range(4):
        lanes = slice(tile * 128, tile * 128 + 128)
        packed[:, :, lanes] = dot(choose, both[:, lanes]).astype(BF16).reshape(SLOTS, 16, 128)
    last = dot(choose, both[:, 512:WIDE])
    packed[:, :, 512:WIDE] = jnp.where(lane < 64, last, bias).astype(BF16).reshape(SLOTS, 16, 128)

    def a_copy(m):
        return pltpu.make_async_remote_copy(
            src_ref=packed.at[m], dst_ref=pages_in.at[core, x, m],
            send_sem=a_send.at[m], recv_sem=a_recv.at[m],
            device_id=target(m), device_id_type=MESH,
        )

    own_copy = pltpu.make_async_copy(packed.at[0], pages_in.at[core, x, 0], own_sem)
    pl.when(core == 1)(lambda: a_copy(0).start())
    pl.when(core == 0)(lambda: own_copy.start())
    for m in range(1, SLOTS):
        a_copy(m).start()

    def resident_keys():
        for i in range(5, len(fetches)):
            fetches[i].wait()
        held = jnp.zeros((16, 64), F32)
        page_ids = iota((16, 64), 0)
        for j in range(8):
            left_over = jnp.clip(res_lengths[...].astype(F32) - 64.0 * j, 0.0, 64.0)
            held = held + jnp.where(tables[j : j + 1, :] == page_ids, left_over, 0.0)
        shift = jnp.where(iota((64, 128), 0) == iota((64, 128), 1) - 64, 1.0, 0.0).astype(BF16)
        held = dot(held.astype(BF16), shift).astype(BF16)
        spread = jnp.where(iota((1024, 16), 0) // 64 == iota((1024, 16), 1), 1.0, 0.0).astype(BF16)
        held = dot(spread, held)
        place = (iota((1024, 128), 0) % 64).astype(F32)
        lane = iota((1024, 128), 1)
        bias = jnp.where((place < held) | (lane < 64), 0.0, -BIG)
        res_keys[0:1024, 512:WIDE] = bias.astype(BF16)
        res_keys[0:1024, 512:LAT] = pool_codes[:, 512:LAT]
        eye = jnp.where(iota((64, 64), 0) == iota((64, 64), 1), 1.0, 0.0).astype(BF16)
        for p in range(16):
            at = slice(p * 64, p * 64 + 64)
            scale_map = dot_t(eye, spread_scales(pool_scales[p]))
            res_keys[at, 0:512] = (pool_codes[at, 0:512].astype(F32) * scale_map).astype(BF16)
        same = iota((128, 128), 0) % 64 == iota((128, 128), 1) - 64
        res_keys[1024:1152, 512:WIDE] = jnp.where(same, 0.0, -BIG).astype(BF16)
        res_keys[1024:1152, 0:LAT] = fresh[...]
        row_of = (iota((1024, 128), 0) // 8) % 64
        wide_q[:, 512:WIDE] = jnp.where(row_of == iota((1024, 128), 1) - 64, 1.0, 0.0).astype(BF16)
        wide_q[:, 0:LAT] = queries[...]

    def resident_block(block):
        rows_at = slice(block * 128, block * 128 + 128)
        query = wide_q[rows_at, :]
        scores = dot_t(query, res_keys[0:1024, :])
        fresh_scores = dot_t(query, res_keys[1024:1152, :])
        if block < 4:
            fresh_scores = jnp.where(iota((128, 128), 1) < 64, fresh_scores, -BIG)
        mixed = softmax_mix(
            scores, fresh_scores, res_keys[0:1024, 0:512], res_keys[1024:1152, 0:512]
        ).astype(F32)
        for tile in range(4):
            lat[tile, rows_at, :] = mixed[:, tile * 128 : tile * 128 + 128]

    def hop(src_x, span, q, sems, device):
        send, recv = sems
        ref = pages_in.at[core, src_x, pl.ds(span[0], span[1] - span[0])]
        return pltpu.make_async_remote_copy(
            src_ref=ref, dst_ref=ref, send_sem=send.at[q], recv_sem=recv.at[q],
            device_id=device, device_id_type=MESH,
        )

    def to_partner(src_x, q, which, from_core):
        span = GROUPS[q]
        ref = pages_in.at[from_core, src_x, pl.ds(span[0], span[1] - span[0])]
        return pltpu.make_async_remote_copy(
            src_ref=ref, dst_ref=ref, send_sem=p_send.at[q, which], recv_sem=p_recv.at[q, which],
            device_id=partner, device_id_type=MESH,
        )

    right_sems, left_sems = (r_send, r_recv), (l_send, l_recv)
    far_right, far_left = (rr_send, rr_recv), (ll_send, ll_recv)

    def halves(q):
        first, last = GROUPS[q]
        return (first, (first + last) // 2), ((first + last) // 2, last)

    def sent(q):
        yield hop(x, GROUPS[q], q, right_sems, right)
        yield hop(x, GROUPS[q], q, left_sems, left)
        if q == LAST:
            yield hop(x, GROUPS[q], q, far_right, far)
        else:
            yield hop(left_x, halves(q)[0], q, far_right, right)
            yield hop(right_x, halves(q)[1], q, far_left, left)

    def stage_own(q):
        for m in range(*GROUPS[q]):
            if m == 0:
                pl.when(core == 1)(lambda: a_copy(0).wait_recv())
                pl.when(core == 0)(lambda: own_copy.wait())
            else:
                a_copy(m).wait_recv()
        hop(x, GROUPS[q], q, right_sems, right).start()
        hop(x, GROUPS[q], q, left_sems, left).start()
        if q == LAST:
            hop(x, GROUPS[q], q, far_right, far).start()
        to_partner(x, q, 0, core).start()

    def stage_near(q):
        hop(left_x, GROUPS[q], q, right_sems, right).wait_recv()
        if q != LAST:
            hop(left_x, halves(q)[0], q, far_right, right).start()
        to_partner(left_x, q, 1, core).start()
        hop(right_x, GROUPS[q], q, left_sems, left).wait_recv()
        if q != LAST:
            hop(right_x, halves(q)[1], q, far_left, left).start()
        to_partner(right_x, q, 2, core).start()

    def stage_far(q):
        if q == LAST:
            hop(far_x, GROUPS[q], q, far_right, far).wait_recv()
        else:
            hop(far_x, halves(q)[0], q, far_right, right).wait_recv()
            hop(far_x, halves(q)[1], q, far_left, left).wait_recv()
        to_partner(far_x, q, 3, core).start()

    def stage_done(q):
        for which, src_x in enumerate((x, left_x, right_x, far_x)):
            to_partner(src_x, q, which, 1 - core).wait_recv()

    resident_keys()
    steps = len(GROUPS)
    for step in range(steps + 3):
        if step < 8:
            resident_block(step)
        if step < steps:
            stage_own(step)
        if 1 <= step < steps + 1:
            stage_near(step - 1)
        if 2 <= step < steps + 2:
            stage_far(step - 2)
        if 3 <= step:
            stage_done(step - 3)

    slots = 2 * SLOTS
    tail = pages_in[:, 0, :, :, 512:WIDE].reshape(slots * 16, 128)
    heads_of = jnp.where(iota((slots, slots * 16), 1) == iota((slots, slots * 16), 0) * 16, 1.0, 0.0)
    marks = dot(heads_of.astype(BF16), tail)
    k_of = iota((slots, 128), 0)
    marks = jnp.where(iota((slots, 128), 1) == 64 + k_of % 4, marks, -BIG)
    present = jnp.where(jnp.max(marks, axis=1, keepdims=True) > -1.0, 1.0, 0.0)

    def owner_of(k):
        dz, dy = slot_offset(k % SLOTS, k // SLOTS)
        return ((z + NZ - dz) % NZ) * NY + (y + 2 * NY - dy) % NY

    eye = iota((slots, slots), 0) == iota((slots, slots), 1)
    present_row = dot(jnp.ones((slots, slots), BF16), jnp.where(eye, present, 0.0).astype(BF16))
    before = owner_of(iota((slots, slots), 1)) < owner_of(iota((slots, slots), 0))
    rank = jnp.sum(jnp.where(before, present_row, 0.0), axis=1, keepdims=True)
    arrivals = jnp.sum(present_row[0:8, :], axis=1, keepdims=True)[0:1, :]
    rank = jnp.where(present > 0.5, rank, -1.0)
    slot_rows = slots * 8
    widen = jnp.where(iota((slot_rows, slots), 0) // 8 == iota((slot_rows, slots), 1), 1.0, 0.0)
    rank_col = dot(widen.astype(BF16), jnp.broadcast_to(rank, (slots, 128)).astype(BF16))[:, 0:1]
    head_col = (iota((slot_rows, 1), 0) % 8).astype(F32)
    goal_col = jnp.where(rank_col > -0.5, rank_col * 8.0 + head_col, -1.0).astype(I32)
    to_slots = jnp.where(goal_col == iota((slot_rows, 512), 1), 1.0, 0.0).astype(BF16)
    narrow = jnp.where(iota((slots, slot_rows), 1) // 8 == iota((slots, slot_rows), 0), rank, 0.0)
    rank_row = dot(jnp.ones((8, slots), BF16), narrow.astype(BF16))[0:1, :]
    head_row = (iota((1, slot_rows), 1) % 8).astype(F32)
    goal_row = jnp.where(rank_row > -0.5, rank_row * 8.0 + head_row, -1.0).astype(I32)
    to_rows = jnp.where(goal_row == iota((512, slot_rows), 0), 1.0, 0.0).astype(BF16)
    fresh_pick = jnp.where(rank.astype(I32) == iota((slots, 64), 1), 1.0, 0.0).astype(BF16)
    slot_fresh[:, 512:WIDE] = jnp.zeros((2 * slots, 128), BF16)
    for j in range(2):
        slot_fresh[j * slots : (j + 1) * slots, 0:LAT] = dot(
            fresh_pick, fresh[j * 64 : j * 64 + 64, :]
        ).astype(BF16)
    for s in range(2):
        at = slice(s * slot_rows, (s + 1) * slot_rows)
        got = dot(to_slots, wide_q[s * 512 : s * 512 + 512, :])
        slot_q[at, 0:512] = got[:, 0:512].astype(BF16)
        lane = iota((slot_rows, 128), 1)
        mark = jnp.where(lane - 64 == (iota((slot_rows, 128), 0) // 8) % 4, 1.0, 0.0)
        slot_q[at, 512:WIDE] = jnp.where(lane < 64, got[:, 512:WIDE], mark).astype(BF16)

    def arrived_block(block):
        slot = block % (BLOCKS // 2) * 4
        page_keys = pages_in[block // (BLOCKS // 2), :, slot : slot + 4].reshape(256, WIDE)
        query = jnp.concatenate(
            [
                slot_q[block * 32 : block * 32 + 32, :],
                slot_q[slot_rows + block * 32 : slot_rows + block * 32 + 32, :],
            ],
            axis=0,
        )
        scores = dot_t(query, page_keys)
        fresh_scores = dot_t(query, slot_fresh[...])
        row = iota((64, 2 * slots), 0)
        lane = iota((64, 2 * slots), 1)
        step = row // 32
        slot = block * 4 + (row % 32) // 8
        fresh_ok = (lane % slots == slot) & (lane // slots <= step)
        fresh_scores = jnp.where(fresh_ok, fresh_scores, -BIG)
        mixed = softmax_mix(scores, fresh_scores, page_keys[:, 0:512], slot_fresh[:, 0:512])
        slot_lat[block * 32 : block * 32 + 32, :] = mixed[0:32]
        slot_lat[slot_rows + block * 32 : slot_rows + block * 32 + 32, :] = mixed[32:64]

    for block in range(BLOCKS):
        arrived_block(block)

    resident_row = (iota((512, 1), 0) // 8).astype(F32) >= arrivals
    for s in range(2):
        rows_at = slice(s * 512, s * 512 + 512)
        moved = dot(to_rows, slot_lat[s * slot_rows : (s + 1) * slot_rows, :])
        for tile in range(4):
            part = moved[:, tile * 128 : tile * 128 + 128]
            lat[tile, rows_at, :] = jnp.where(resident_row, lat[tile, rows_at, :], part)
    for h in range(8):
        per_head = jnp.concatenate(
            [lat[tile, pl.ds(h, 128, stride=8), :].astype(BF16) for tile in range(4)], axis=1
        )
        out[:, h * 128 : h * 128 + 128] = dot(per_head, projection[h]).astype(BF16)

    for q in range(steps):
        for copy in sent(q):
            copy.wait_send()
        for which, src_x in enumerate((x, left_x, right_x, far_x)):
            to_partner(src_x, q, which, core).wait_send()
    pl.when(core == 1)(lambda: a_copy(0).wait_send())
    for m in range(1, SLOTS):
        a_copy(m).wait_send()


def shards(
    prefill_codes, prefill_scales, page_lists, req_lengths, destinations, pool_codes, pool_scales,
    res_tables, res_lengths, queries, new_latents, value_projection,
):
    slots = 2 * SLOTS
    dma = pltpu.SemaphoreType.DMA
    operands = (
        prefill_codes.reshape(256, LAT),
        jnp.transpose(prefill_scales, (1, 2, 0)),
        page_lists.reshape(1, 32),
        req_lengths.reshape(1, 32),
        destinations.reshape(1, 32),
        pool_codes.reshape(1024, LAT),
        jnp.transpose(pool_scales, (0, 2, 1)),
        jnp.transpose(res_tables),
        res_lengths.reshape(1, 64),
        queries.reshape(1024, LAT),
        new_latents.reshape(128, LAT),
        value_projection,
    )
    groups = dma((len(GROUPS),))
    result = pl.pallas_call(
        kernel,
        out_shape=jax.ShapeDtypeStruct((128, 1024), BF16),
        in_specs=[pl.BlockSpec(memory_space=pltpu.HBM)] * 12,
        out_specs=pl.BlockSpec(memory_space=pltpu.VMEM),
        scratch_shapes=[pltpu.VMEM(item.shape, item.dtype) for item in operands]
        + [
            pltpu.VMEM((2, 256, WIDE), BF16),
            pltpu.VMEM((SLOTS, 16, WIDE), BF16),
            pltpu.VMEM((2, NX, SLOTS, 16, WIDE), BF16),
            pltpu.VMEM((1152, WIDE), BF16),
            pltpu.VMEM((1024, WIDE), BF16),
            pltpu.VMEM((2 * slots * 8, WIDE), BF16),
            pltpu.VMEM((2 * slots, WIDE), BF16),
            pltpu.VMEM((2 * slots * 8, 512), BF16),
            pltpu.VMEM((4, 1024, 128), F32),
            dma((12,)), dma, dma, dma((SLOTS,)), dma((SLOTS,)),
            groups, groups, groups, groups, groups, groups, groups, groups,
            dma((len(GROUPS), 4)), dma((len(GROUPS), 4)), dma,
        ],
        compiler_params=pltpu.CompilerParams(
            collective_id=0, has_side_effects=True, vmem_limit_bytes=64 * 1024 * 1024
        ),
    )(*operands)
    return result.reshape(2, 64, 1024)


def solution(mesh):
    return jax.shard_map(
        shards,
        mesh=mesh,
        in_specs=(
            P("inst", "head", None),
            P("inst", "head", None),
            P("inst", None),
            P("inst"),
            P("inst"),
            P("inst", None, None),
            P("inst", None, None),
            P("inst", None),
            P("inst"),
            P(None, "inst", "head", None),
            P(None, "inst", None),
            P("head", None, None),
        ),
        out_specs=P(None, "inst", "head"),
        check_vma=False,
    )
```

```python
import functools
import math

import jax
import jax.numpy as jnp
from jax import lax
from jax.experimental import pallas as pl
from jax.experimental.pallas import tpu as pltpu
from jax.sharding import PartitionSpec as P

LATENT_WIDTH = 512
LAT = 576
WIDE = 640
NZ, NY, NX = 16, 4, 4
SLOTS = NZ * NY // 2
BLOCKS = 2 * SLOTS // 4
GROUPS = ((0, 6), (6, 10), (10, 14), (14, 18), (18, 22), (22, 26), (26, 30), (30, 32))
LAST = len(GROUPS) - 1
BIG = 1e30
MESH = pl.DeviceIdType.MESH
softmax_scale = (0.1 * math.log(40.0) + 1.0) ** 2 / math.sqrt(192.0)
F32, BF16, I32 = jnp.float32, jnp.bfloat16, jnp.int32


def iota(shape, axis):
    return lax.broadcasted_iota(I32, shape, axis)


def dot(a, b):
    return lax.dot_general(a, b, (((1,), (0,)), ((), ())), preferred_element_type=F32)


def dot_t(a, b):
    return lax.dot_general(a, b, (((1,), (1,)), ((), ())), preferred_element_type=F32)


def slot_offset(m, core):
    pair = m // 2
    if isinstance(m, int):
        dz = (pair + 1) // 2 if pair % 2 else (NZ - pair // 2) % NZ
    else:
        dz = jnp.where(pair % 2 == 1, (pair + 1) // 2, (NZ - pair // 2) % NZ)
    return dz, 2 * (m % 2) + core


def spread_scales(scales):
    n = scales.shape[1]
    scales = scales.astype(F32)
    spread = [jnp.broadcast_to(scales[j : j + 1, :], (128, n)) for j in range(4)]
    return jnp.concatenate(spread, axis=0).astype(BF16)


def softmax_mix(scores, fresh_scores, values, fresh_values):
    scores = scores * softmax_scale
    fresh_scores = fresh_scores * softmax_scale
    highest = jnp.maximum(
        jnp.max(scores, axis=1, keepdims=True), jnp.max(fresh_scores, axis=1, keepdims=True)
    )
    weights = jnp.exp(scores - highest)
    fresh_weights = jnp.exp(fresh_scores - highest)
    total = jnp.sum(weights, axis=1, keepdims=True) + jnp.sum(fresh_weights, axis=1, keepdims=True)
    mixed = dot(weights.astype(BF16), values) + dot(fresh_weights.astype(BF16), fresh_values)
    return (mixed / total).astype(BF16)


def kernel(
    codes_hbm, scales_hbm, pages_hbm, lengths_hbm, dests_hbm, pool_codes_hbm, pool_scales_hbm,
    tables_hbm, res_lengths_hbm, queries_hbm, fresh_hbm, projection_hbm, out,
    codes, scales, pages, lengths, dests, pool_codes, pool_scales,
    tables, res_lengths, queries, fresh, projection,
    keys, packed, pages_in, res_keys, wide_q, slot_q, slot_fresh, slot_lat, lat,
    meta, meta_in, slot_out, res_out,
    in_sems, key_send, key_recv, a_send, a_recv, r_send, r_recv, l_send, l_recv,
    rr_send, rr_recv, ll_send, ll_recv, p_send, p_recv, own_sem,
    m_send, m_recv, g_send, g_recv, meta_sem,
):
    sources = (
        codes_hbm, scales_hbm, pages_hbm, lengths_hbm, dests_hbm, pool_codes_hbm, pool_scales_hbm,
        tables_hbm, res_lengths_hbm, queries_hbm, fresh_hbm, projection_hbm,
    )
    places = (
        codes, scales, pages, lengths, dests, pool_codes, pool_scales,
        tables, res_lengths, queries, fresh, projection,
    )
    fetches = [
        pltpu.make_async_copy(src, dst, in_sems.at[i])
        for i, (src, dst) in enumerate(zip(sources, places))
    ]
    for i in range(5):
        fetches[i].start()
    inst, head = lax.axis_index("inst"), lax.axis_index("head")
    z, y = inst // NY, inst % NY
    x, core = head // 2, head % 2
    right_x, left_x, far_x = (x + 1) % NX, (x + NX - 1) % NX, (x + 2) % NX
    right, left, far = (inst, right_x * 2 + core), (inst, left_x * 2 + core), (inst, far_x * 2 + core)
    partner = (inst, x * 2 + 1 - core)

    def target(m):
        dz, dy = slot_offset(m, core)
        return (((z + dz) % NZ) * NY + (y + dy) % NY, head)

    target_of = target

    barrier = pltpu.get_barrier_semaphore()
    for device in (partner, right, left, far):
        pl.semaphore_signal(barrier, inc=1, device_id=device, device_id_type=MESH)
    for m in range(SLOTS):
        if m == 0:
            @pl.when(core == 1)
            def _():
                pl.semaphore_signal(barrier, inc=1, device_id=target(0), device_id_type=MESH)
        else:
            pl.semaphore_signal(barrier, inc=1, device_id=target(m), device_id_type=MESH)

    for i in range(5, len(fetches)):
        fetches[i].start()

    own = keys.at[core]
    own[:, 512:WIDE] = jnp.zeros((256, 128), BF16)
    fetches[0].wait()
    fetches[1].wait()
    token_row = iota((256, 32), 0)
    of_page = token_row // 8 == iota((256, 32), 1)
    scale_map = jnp.zeros((256, 512), F32)
    for t in range(8):
        at_token = jnp.where(of_page & (token_row % 8 == t), 1.0, 0.0).astype(BF16)
        scale_map = scale_map + dot_t(at_token, spread_scales(scales[t]))
    own[:, 0:512] = (codes[:, 0:512].astype(F32) * scale_map).astype(BF16)
    own[:, 512:LAT] = codes[:, 512:LAT]
    for i in range(2, 5):
        fetches[i].wait()

    pl.semaphore_wait(barrier, SLOTS + 3 + core)
    key_copy = pltpu.make_async_remote_copy(
        src_ref=own, dst_ref=own, send_sem=key_send, recv_sem=key_recv,
        device_id=partner, device_id_type=MESH,
    )
    key_copy.start()

    rows = SLOTS * 16
    row = iota((rows, 32), 0)
    dz, dy = slot_offset(row // 16, core)
    wanted = ((z + dz) % NZ) * NY + (y + dy) % NY
    hit = dests[...] == wanted
    page = jnp.sum(jnp.where(hit, pages[...].astype(F32) + 1.0, 0.0), axis=1, keepdims=True)
    marks = jnp.broadcast_to(jnp.where(page > 0.5, 1.0, 0.0), (rows, 128))
    meta[...] = marks.reshape(SLOTS, 2, 8, 128)[:, 0]

    def meta_copy(a):
        return pltpu.make_async_remote_copy(
            src_ref=meta.at[4 * a + x], dst_ref=meta_in.at[core, x, a],
            send_sem=m_send.at[a], recv_sem=m_recv.at[a],
            device_id=target_of(4 * a + x), device_id_type=MESH,
        )

    def meta_own():
        return pltpu.make_async_copy(meta.at[0], meta_in.at[core, x, 0], meta_sem)

    to_self = (core == 0) & (x == 0)
    pl.when(jnp.logical_not(to_self))(lambda: meta_copy(0).start())
    pl.when(to_self)(lambda: meta_own().start())
    for a in range(1, SLOTS // NX):
        meta_copy(a).start()

    def meta_gather(i):
        ref = meta_in.at[core, x]
        return pltpu.make_async_remote_copy(
            src_ref=ref, dst_ref=ref, send_sem=g_send.at[i], recv_sem=g_recv.at[i],
            device_id=(right, left, far)[i], device_id_type=MESH,
        )

    def meta_partner(from_core):
        ref = meta_in.at[from_core]
        return pltpu.make_async_remote_copy(
            src_ref=ref, dst_ref=ref, send_sem=g_send.at[3], recv_sem=g_recv.at[3],
            device_id=partner, device_id_type=MESH,
        )

    count = jnp.sum(jnp.where(hit, lengths[...].astype(F32), 0.0), axis=1, keepdims=True)
    slot_row = iota((rows, 1), 0)
    token = slot_row % 16
    column = (token // 8) * 256 + (page.astype(I32) - 1) * 8 + token % 8
    column = jnp.where(page > 0.5, column, -1)
    choose = jnp.where(column == iota((rows, 512), 1), 1.0, 0.0).astype(BF16)
    valid = (x * 16 + token).astype(F32) < count
    lane = iota((rows, 128), 1)
    mine = (lane - 64) == (slot_row // 16) % 4
    bias = jnp.where(lane < 68, jnp.where(mine & valid, 0.0, -BIG), 0.0)

    key_copy.wait()
    both = keys[...].reshape(512, WIDE)
    for tile in range(4):
        lanes = slice(tile * 128, tile * 128 + 128)
        packed[:, :, lanes] = dot(choose, both[:, lanes]).astype(BF16).reshape(SLOTS, 16, 128)
    last = dot(choose, both[:, 512:WIDE])
    packed[:, :, 512:WIDE] = jnp.where(lane < 64, last, bias).astype(BF16).reshape(SLOTS, 16, 128)

    def a_copy(m):
        return pltpu.make_async_remote_copy(
            src_ref=packed.at[m], dst_ref=pages_in.at[core, x, m],
            send_sem=a_send.at[m], recv_sem=a_recv.at[m],
            device_id=target(m), device_id_type=MESH,
        )

    own_copy = pltpu.make_async_copy(packed.at[0], pages_in.at[core, x, 0], own_sem)
    pl.when(core == 1)(lambda: a_copy(0).start())
    pl.when(core == 0)(lambda: own_copy.start())
    for m in range(1, SLOTS):
        a_copy(m).start()

    def resident_keys():
        for i in range(5, len(fetches)):
            fetches[i].wait()
        held = jnp.zeros((16, 64), F32)
        page_ids = iota((16, 64), 0)
        for j in range(8):
            left_over = jnp.clip(res_lengths[...].astype(F32) - 64.0 * j, 0.0, 64.0)
            held = held + jnp.where(tables[j : j + 1, :] == page_ids, left_over, 0.0)
        shift = jnp.where(iota((64, 128), 0) == iota((64, 128), 1) - 64, 1.0, 0.0).astype(BF16)
        held = dot(held.astype(BF16), shift).astype(BF16)
        spread = jnp.where(iota((1024, 16), 0) // 64 == iota((1024, 16), 1), 1.0, 0.0).astype(BF16)
        held = dot(spread, held)
        place = (iota((1024, 128), 0) % 64).astype(F32)
        lane = iota((1024, 128), 1)
        bias = jnp.where((place < held) | (lane < 64), 0.0, -BIG)
        res_keys[0:1024, 512:WIDE] = bias.astype(BF16)
        res_keys[0:1024, 512:LAT] = pool_codes[:, 512:LAT]
        eye = jnp.where(iota((64, 64), 0) == iota((64, 64), 1), 1.0, 0.0).astype(BF16)
        for p in range(16):
            at = slice(p * 64, p * 64 + 64)
            scale_map = dot_t(eye, spread_scales(pool_scales[p]))
            res_keys[at, 0:512] = (pool_codes[at, 0:512].astype(F32) * scale_map).astype(BF16)
        same = iota((128, 128), 0) % 64 == iota((128, 128), 1) - 64
        res_keys[1024:1152, 512:WIDE] = jnp.where(same, 0.0, -BIG).astype(BF16)
        res_keys[1024:1152, 0:LAT] = fresh[...]
        row_of = (iota((1024, 128), 0) // 8) % 64
        wide_q[:, 512:WIDE] = jnp.where(row_of == iota((1024, 128), 1) - 64, 1.0, 0.0).astype(BF16)
        wide_q[:, 0:LAT] = queries[...]

    def resident_block(block):
        rows_at = slice(block * 128, block * 128 + 128)
        query = wide_q[rows_at, :]
        scores = dot_t(query, res_keys[0:1024, :])
        fresh_scores = dot_t(query, res_keys[1024:1152, :])
        if block < 4:
            fresh_scores = jnp.where(iota((128, 128), 1) < 64, fresh_scores, -BIG)
        mixed = softmax_mix(
            scores, fresh_scores, res_keys[0:1024, 0:512], res_keys[1024:1152, 0:512]
        ).astype(F32)
        for tile in range(4):
            lat[tile, rows_at, :] = mixed[:, tile * 128 : tile * 128 + 128]

    def hop(src_x, span, q, sems, device):
        send, recv = sems
        ref = pages_in.at[core, src_x, pl.ds(span[0], span[1] - span[0])]
        return pltpu.make_async_remote_copy(
            src_ref=ref, dst_ref=ref, send_sem=send.at[q], recv_sem=recv.at[q],
            device_id=device, device_id_type=MESH,
        )

    def to_partner(src_x, q, which, from_core):
        span = GROUPS[q]
        ref = pages_in.at[from_core, src_x, pl.ds(span[0], span[1] - span[0])]
        return pltpu.make_async_remote_copy(
            src_ref=ref, dst_ref=ref, send_sem=p_send.at[q, which], recv_sem=p_recv.at[q, which],
            device_id=partner, device_id_type=MESH,
        )

    right_sems, left_sems = (r_send, r_recv), (l_send, l_recv)
    far_right, far_left = (rr_send, rr_recv), (ll_send, ll_recv)

    def halves(q):
        first, last = GROUPS[q]
        return (first, (first + last) // 2), ((first + last) // 2, last)

    def sent(q):
        yield hop(x, GROUPS[q], q, right_sems, right)
        yield hop(x, GROUPS[q], q, left_sems, left)
        if True:
            yield hop(x, GROUPS[q], q, far_right, far)
        else:
            yield hop(left_x, halves(q)[0], q, far_right, right)
            yield hop(right_x, halves(q)[1], q, far_left, left)

    def stage_own(q):
        for m in range(*GROUPS[q]):
            if m == 0:
                pl.when(core == 1)(lambda: a_copy(0).wait_recv())
                pl.when(core == 0)(lambda: own_copy.wait())
            else:
                a_copy(m).wait_recv()
        hop(x, GROUPS[q], q, right_sems, right).start()
        hop(x, GROUPS[q], q, left_sems, left).start()
        if True:
            hop(x, GROUPS[q], q, far_right, far).start()
        to_partner(x, q, 0, core).start()

    def stage_near(q):
        hop(left_x, GROUPS[q], q, right_sems, right).wait_recv()
        to_partner(left_x, q, 1, core).start()
        hop(right_x, GROUPS[q], q, left_sems, left).wait_recv()
        to_partner(right_x, q, 2, core).start()

    def stage_far(q):
        if True:
            hop(far_x, GROUPS[q], q, far_right, far).wait_recv()
        else:
            hop(far_x, halves(q)[0], q, far_right, right).wait_recv()
            hop(far_x, halves(q)[1], q, far_left, left).wait_recv()
        to_partner(far_x, q, 3, core).start()

    def stage_done(q):
        for which, src_x in enumerate((x, left_x, right_x, far_x)):
            to_partner(src_x, q, which, 1 - core).wait_recv()

    slots = 2 * SLOTS

    def meta_first():
        pl.when(jnp.logical_not(to_self))(lambda: meta_copy(0).wait_recv())
        pl.when(to_self)(lambda: meta_own().wait())
        for a in range(1, SLOTS // NX):
            meta_copy(a).wait_recv()
        for i in range(3):
            meta_gather(i).start()

    def meta_second():
        for i in range(3):
            meta_gather(i).wait_recv()
        meta_partner(core).start()

    def owner_of(k):
        dz, dy = slot_offset(k % SLOTS, k // SLOTS)
        return ((z + NZ - dz) % NZ) * NY + (y + 2 * NY - dy) % NY

    def slot_rows_of():
        meta_partner(1 - core).wait_recv()
        k = iota((slots, slots * 8), 0)
        at = ((k // SLOTS) * SLOTS + (k % 4) * (SLOTS // 4) + (k % SLOTS) // 4) * 8
        pick = jnp.where(iota((slots, slots * 8), 1) == at, 1.0, 0.0).astype(BF16)
        present = dot(pick, meta_in[...].reshape(slots * 8, 128).astype(BF16))[:, 0:1]
        eye = iota((slots, slots), 0) == iota((slots, slots), 1)
        present_row = dot(jnp.ones((slots, slots), BF16), jnp.where(eye, present, 0.0).astype(BF16))
        before = owner_of(iota((slots, slots), 1)) < owner_of(iota((slots, slots), 0))
        rank = jnp.sum(jnp.where(before, present_row, 0.0), axis=1, keepdims=True)
        arrivals = jnp.sum(present_row[0:8, :], axis=1, keepdims=True)[0:1, :]
        rank = jnp.where(present > 0.5, rank, -1.0)
        ranks = jnp.broadcast_to(rank, (slots, 128)).astype(BF16)
        widen = jnp.where(iota((512, slots), 0) // 8 == iota((512, slots), 1), 1.0, 0.0)
        rank_col = dot(widen.astype(BF16), ranks)[:, 0:1]
        head_col = (iota((512, 1), 0) % 8).astype(F32)
        goal_col = jnp.where(rank_col > -0.5, rank_col * 8.0 + head_col, -1.0).astype(I32)
        to_slots = jnp.where(goal_col == iota((512, 512), 1), 1.0, 0.0).astype(BF16)
        fresh_pick = jnp.where(rank.astype(I32) == iota((slots, 64), 1), 1.0, 0.0).astype(BF16)
        slot_fresh[:, 512:WIDE] = jnp.zeros((2 * slots, 128), BF16)
        for j in range(2):
            slot_fresh[j * slots : (j + 1) * slots, 0:LAT] = dot(
                fresh_pick, fresh[j * 64 : j * 64 + 64, :]
            ).astype(BF16)
        lane = iota((512, 128), 1)
        mark = jnp.where(lane - 64 == (iota((512, 128), 0) // 8) % 4, 1.0, 0.0)
        for s in range(2):
            got = dot(to_slots, wide_q[s * 512 : s * 512 + 512, :])
            slot_q[:, s, :, 0:512] = got[:, 0:512].astype(BF16).reshape(BLOCKS, 32, 512)
            last = jnp.where(lane < 64, got[:, 512:WIDE], mark).astype(BF16)
            slot_q[:, s, :, 512:WIDE] = last.reshape(BLOCKS, 32, 128)
        n = iota((slots, 128), 1)
        spot = jnp.where(n // 8 * 4 + n % 4 == iota((slots, 128), 0), rank, 0.0)
        rank_row = dot(jnp.ones((8, slots), BF16), spot.astype(BF16))[0:1, :]
        n = iota((128, 128), 1)
        row = iota((128, 128), 0)
        same = (rank_row.astype(I32) == row % 64) & (n // 4 % 2 == row // 64)
        return jnp.where(same, 1.0, 0.0).astype(BF16), arrivals

    def arrived_blocks(*blocks):
        queries_of = [slot_q[block].reshape(64, WIDE) for block in blocks]
        keys_of = []
        for block in blocks:
            at = block % (BLOCKS // 2) * 4
            keys_of.append(pages_in[block // (BLOCKS // 2), :, at : at + 4].reshape(256, WIDE))
        row, lane = iota((64, 2 * slots), 0), iota((64, 2 * slots), 1)
        results = []
        for block, query, page_keys in zip(blocks, queries_of, keys_of):
            scores = dot_t(query, page_keys)
            fresh_scores = dot_t(query, slot_fresh[...])
            slot = block * 4 + (row % 32) // 8
            fresh_ok = (lane % slots == slot) & (lane // slots <= row // 32)
            results.append((scores, jnp.where(fresh_ok, fresh_scores, -BIG)))
        for block, page_keys, (scores, fresh_scores) in zip(blocks, keys_of, results):
            mixed = softmax_mix(scores, fresh_scores, page_keys[:, 0:512], slot_fresh[:, 0:512])
            mixed = mixed.astype(F32)
            for tile in range(4):
                slot_lat[tile, block * 64 : block * 64 + 64, :] = mixed[:, tile * 128 : tile * 128 + 128]

    def project(source, start, count):
        results = []
        for h in range(8):
            at = pl.ds(start * 8 + h, count, stride=8)
            per_head = jnp.concatenate([source[t, at, :].astype(BF16) for t in range(4)], axis=1)
            results.append(dot(per_head, projection[h]).astype(BF16))
        return jnp.concatenate(results, axis=1)

    resident_keys()
    steps = len(GROUPS)
    for step in range(steps + 3):
        if step < 8:
            resident_block(step)
        if step < steps:
            stage_own(step)
        if 1 <= step < steps + 1:
            stage_near(step - 1)
        if 2 <= step < steps + 2:
            stage_far(step - 2)
        if step == 0:
            meta_first()
        if step == 1:
            meta_second()
        if step == 2:
            to_rows, arrivals = slot_rows_of()
        if step == 8:
            res_out[...] = project(lat, 0, 128)
        if 3 <= step:
            stage_done(step - 3)
            block = step - 3
            arrived_blocks(block, block + BLOCKS // 2)
            half = BLOCKS // 2
            if block == half - 2:
                slot_out[0:56, :] = project(slot_lat, 0, 56)
                slot_out[64:120, :] = project(slot_lat, 64, 56)
            if block == half - 1:
                slot_out[56:64, :] = project(slot_lat, 56, 8)
                slot_out[120:128, :] = project(slot_lat, 120, 8)

    moved = dot(to_rows, slot_out[...])
    resident_row = (iota((128, 1), 0) % 64).astype(F32) >= arrivals
    out[...] = jnp.where(resident_row, res_out[...].astype(F32), moved).astype(BF16)

    pl.when(jnp.logical_not(to_self))(lambda: meta_copy(0).wait_send())
    for a in range(1, SLOTS // NX):
        meta_copy(a).wait_send()
    for i in range(3):
        meta_gather(i).wait_send()
    meta_partner(core).wait_send()
    for q in range(steps):
        for copy in sent(q):
            copy.wait_send()
        for which, src_x in enumerate((x, left_x, right_x, far_x)):
            to_partner(src_x, q, which, core).wait_send()
    pl.when(core == 1)(lambda: a_copy(0).wait_send())
    for m in range(1, SLOTS):
        a_copy(m).wait_send()


def shards(
    prefill_codes, prefill_scales, page_lists, req_lengths, destinations, pool_codes, pool_scales,
    res_tables, res_lengths, queries, new_latents, value_projection,
):
    slots = 2 * SLOTS
    dma = pltpu.SemaphoreType.DMA
    operands = (
        prefill_codes.reshape(256, LAT),
        jnp.transpose(prefill_scales, (1, 2, 0)),
        page_lists.reshape(1, 32),
        req_lengths.reshape(1, 32),
        destinations.reshape(1, 32),
        pool_codes.reshape(1024, LAT),
        jnp.transpose(pool_scales, (0, 2, 1)),
        jnp.transpose(res_tables),
        res_lengths.reshape(1, 64),
        queries.reshape(1024, LAT),
        new_latents.reshape(128, LAT),
        value_projection,
    )
    groups = dma((len(GROUPS),))
    result = pl.pallas_call(
        kernel,
        out_shape=jax.ShapeDtypeStruct((128, 1024), BF16),
        in_specs=[pl.BlockSpec(memory_space=pltpu.HBM)] * 12,
        out_specs=pl.BlockSpec(memory_space=pltpu.VMEM),
        scratch_shapes=[pltpu.VMEM(item.shape, item.dtype) for item in operands]
        + [
            pltpu.VMEM((2, 256, WIDE), BF16),
            pltpu.VMEM((SLOTS, 16, WIDE), BF16),
            pltpu.VMEM((2, NX, SLOTS, 16, WIDE), BF16),
            pltpu.VMEM((1152, WIDE), BF16),
            pltpu.VMEM((1024, WIDE), BF16),
            pltpu.VMEM((BLOCKS, 2, 32, WIDE), BF16),
            pltpu.VMEM((2 * slots, WIDE), BF16),
            pltpu.VMEM((4, BLOCKS * 64, 128), F32),
            pltpu.VMEM((4, 1024, 128), F32),
            pltpu.VMEM((SLOTS, 8, 128), F32),
            pltpu.VMEM((2, NX, SLOTS // NX, 8, 128), F32),
            pltpu.VMEM((128, 1024), BF16),
            pltpu.VMEM((128, 1024), BF16),
            dma((12,)), dma, dma, dma((SLOTS,)), dma((SLOTS,)),
            groups, groups, groups, groups, groups, groups, groups, groups,
            dma((len(GROUPS), 4)), dma((len(GROUPS), 4)), dma,
            dma((SLOTS // NX,)), dma((SLOTS // NX,)), dma((4,)), dma((4,)), dma,
        ],
        compiler_params=pltpu.CompilerParams(
            collective_id=0, has_side_effects=True, vmem_limit_bytes=64 * 1024 * 1024
        ),
    )(*operands)
    return result.reshape(2, 64, 1024)


def solution(mesh):
    return jax.shard_map(
        shards,
        mesh=mesh,
        in_specs=(
            P("inst", "head", None),
            P("inst", "head", None),
            P("inst", None),
            P("inst"),
            P("inst"),
            P("inst", None, None),
            P("inst", None, None),
            P("inst", None),
            P("inst"),
            P(None, "inst", "head", None),
            P(None, "inst", None),
            P("head", None, None),
        ),
        out_specs=P(None, "inst", "head"),
        check_vma=False,
    )
```

```python
import functools
import math

import jax
import jax.numpy as jnp
from jax import lax
from jax.experimental import pallas as pl
from jax.experimental.pallas import tpu as pltpu
from jax.sharding import PartitionSpec as P

LATENT_WIDTH = 512
LAT = 576
WIDE = 640
NZ, NY, NX = 16, 4, 4
SLOTS = NZ * NY // 2
BLOCKS = 2 * SLOTS // 4
GROUPS = ((0, 6), (6, 10), (10, 14), (14, 18), (18, 22), (22, 26), (26, 30), (30, 32))
BIG = 1e30
MESH = pl.DeviceIdType.MESH
softmax_scale = (0.1 * math.log(40.0) + 1.0) ** 2 / math.sqrt(192.0)
F32, BF16, I32 = jnp.float32, jnp.bfloat16, jnp.int32


def iota(shape, axis):
    return lax.broadcasted_iota(I32, shape, axis)


def dot(a, b):
    return lax.dot_general(a, b, (((1,), (0,)), ((), ())), preferred_element_type=F32)


def dot_t(a, b):
    return lax.dot_general(a, b, (((1,), (1,)), ((), ())), preferred_element_type=F32)


def slot_offset(m, core):
    pair = m // 2
    if isinstance(m, int):
        dz = (pair + 1) // 2 if pair % 2 else (NZ - pair // 2) % NZ
    else:
        dz = jnp.where(pair % 2 == 1, (pair + 1) // 2, (NZ - pair // 2) % NZ)
    return dz, 2 * (m % 2) + core


def spread_scales(scales):
    n = scales.shape[1]
    scales = scales.astype(F32)
    spread = [jnp.broadcast_to(scales[j : j + 1, :], (128, n)) for j in range(4)]
    return jnp.concatenate(spread, axis=0).astype(BF16)


def softmax_mix(scores, fresh_scores, values, fresh_values):
    scores = scores * softmax_scale
    fresh_scores = fresh_scores * softmax_scale
    highest = jnp.maximum(
        jnp.max(scores, axis=1, keepdims=True), jnp.max(fresh_scores, axis=1, keepdims=True)
    )
    weights = jnp.exp(scores - highest)
    fresh_weights = jnp.exp(fresh_scores - highest)
    total = jnp.sum(weights, axis=1, keepdims=True) + jnp.sum(fresh_weights, axis=1, keepdims=True)
    mixed = dot(weights.astype(BF16), values) + dot(fresh_weights.astype(BF16), fresh_values)
    return (mixed / total).astype(BF16)


def kernel(
    codes_hbm, scales_hbm, pages_hbm, lengths_hbm, dests_hbm, pool_codes_hbm, pool_scales_hbm,
    tables_hbm, res_lengths_hbm, queries_hbm, fresh_hbm, projection_hbm, out,
    codes, scales, pages, lengths, dests, pool_codes, pool_scales,
    tables, res_lengths, queries, fresh, projection,
    keys, packed, pages_in, res_keys, wide_q, slot_q, slot_fresh, slot_lat, lat,
    meta, meta_in, slot_out, res_out,
    in_sems, key_send, key_recv, a_send, a_recv, h_send, h_recv, p_send, p_recv,
    m_send, m_recv, g_send, g_recv, meta_sem,
):
    sources = (
        codes_hbm, scales_hbm, pages_hbm, lengths_hbm, dests_hbm, pool_codes_hbm, pool_scales_hbm,
        tables_hbm, res_lengths_hbm, queries_hbm, fresh_hbm, projection_hbm,
    )
    places = (
        codes, scales, pages, lengths, dests, pool_codes, pool_scales,
        tables, res_lengths, queries, fresh, projection,
    )
    fetches = [
        pltpu.make_async_copy(src, dst, in_sems.at[i])
        for i, (src, dst) in enumerate(zip(sources, places))
    ]
    for i in range(5):
        fetches[i].start()
    inst, head = lax.axis_index("inst"), lax.axis_index("head")
    z, y = inst // NY, inst % NY
    x, core = head // 2, head % 2
    right_x, left_x, far_x = (x + 1) % NX, (x + NX - 1) % NX, (x + 2) % NX
    right, left, far = (inst, right_x * 2 + core), (inst, left_x * 2 + core), (inst, far_x * 2 + core)
    partner = (inst, x * 2 + 1 - core)

    def target(m):
        dz, dy = slot_offset(m, core)
        return (((z + dz) % NZ) * NY + (y + dy) % NY, head)

    target_of = target

    barrier = pltpu.get_barrier_semaphore()
    for device in (partner, right, left, far):
        pl.semaphore_signal(barrier, inc=1, device_id=device, device_id_type=MESH)
    for m in range(SLOTS):
        if m == 0:
            @pl.when(core == 1)
            def _():
                pl.semaphore_signal(barrier, inc=1, device_id=target(0), device_id_type=MESH)
        else:
            pl.semaphore_signal(barrier, inc=1, device_id=target(m), device_id_type=MESH)

    for i in range(5, len(fetches)):
        fetches[i].start()

    own = keys.at[core]
    own[:, 512:WIDE] = jnp.zeros((256, 128), BF16)
    fetches[0].wait()
    fetches[1].wait()
    token_row = iota((256, 32), 0)
    of_page = token_row // 8 == iota((256, 32), 1)
    scale_map = jnp.zeros((256, 512), F32)
    for t in range(8):
        at_token = jnp.where(of_page & (token_row % 8 == t), 1.0, 0.0).astype(BF16)
        scale_map = scale_map + dot_t(at_token, spread_scales(scales[t]))
    own[:, 0:512] = (codes[:, 0:512].astype(F32) * scale_map).astype(BF16)
    own[:, 512:LAT] = codes[:, 512:LAT]
    for i in range(2, 5):
        fetches[i].wait()

    pl.semaphore_wait(barrier, SLOTS + 3 + core)
    key_copy = pltpu.make_async_remote_copy(
        src_ref=own, dst_ref=own, send_sem=key_send, recv_sem=key_recv,
        device_id=partner, device_id_type=MESH,
    )
    key_copy.start()

    rows = SLOTS * 16
    row = iota((rows, 32), 0)
    dz, dy = slot_offset(row // 16, core)
    wanted = ((z + dz) % NZ) * NY + (y + dy) % NY
    hit = dests[...] == wanted
    page = jnp.sum(jnp.where(hit, pages[...].astype(F32) + 1.0, 0.0), axis=1, keepdims=True)
    marks = jnp.broadcast_to(jnp.where(page > 0.5, 1.0, 0.0), (rows, 128))
    meta[...] = marks.reshape(SLOTS, 2, 8, 128)[:, 0]

    def meta_copy(a):
        return pltpu.make_async_remote_copy(
            src_ref=meta.at[4 * a + x], dst_ref=meta_in.at[core, x, a],
            send_sem=m_send.at[a], recv_sem=m_recv.at[a],
            device_id=target_of(4 * a + x), device_id_type=MESH,
        )

    def meta_own():
        return pltpu.make_async_copy(meta.at[0], meta_in.at[core, x, 0], meta_sem)

    to_self = (core == 0) & (x == 0)
    pl.when(jnp.logical_not(to_self))(lambda: meta_copy(0).start())
    pl.when(to_self)(lambda: meta_own().start())
    for a in range(1, SLOTS // NX):
        meta_copy(a).start()

    def meta_gather(i):
        ref = meta_in.at[core, x]
        return pltpu.make_async_remote_copy(
            src_ref=ref, dst_ref=ref, send_sem=g_send.at[i], recv_sem=g_recv.at[i],
            device_id=(right, left, far)[i], device_id_type=MESH,
        )

    def meta_partner(from_core):
        ref = meta_in.at[from_core]
        return pltpu.make_async_remote_copy(
            src_ref=ref, dst_ref=ref, send_sem=g_send.at[3], recv_sem=g_recv.at[3],
            device_id=partner, device_id_type=MESH,
        )

    count = jnp.sum(jnp.where(hit, lengths[...].astype(F32), 0.0), axis=1, keepdims=True)
    slot_row = iota((rows, 1), 0)
    token = slot_row % 16
    column = (token // 8) * 256 + (page.astype(I32) - 1) * 8 + token % 8
    column = jnp.where(page > 0.5, column, -1)
    choose = jnp.where(column == iota((rows, 512), 1), 1.0, 0.0).astype(BF16)
    valid = (x * 16 + token).astype(F32) < count
    lane = iota((rows, 128), 1)
    mine = (lane - 64) == (slot_row // 16) % 4
    bias = jnp.where(lane < 68, jnp.where(mine & valid, 0.0, -BIG), 0.0)

    group_of = [q for q, (first, last) in enumerate(GROUPS) for _ in range(first, last)]

    def a_copy(m):
        return pltpu.make_async_remote_copy(
            src_ref=packed.at[m], dst_ref=pages_in.at[core, x, m],
            send_sem=a_send.at[min(m, 1)], recv_sem=a_recv.at[group_of[m]],
            device_id=target(m), device_id_type=MESH,
        )

    own_copy = pltpu.make_async_copy(packed.at[0], pages_in.at[core, x, 0], a_recv.at[0])
    key_copy.wait()
    both = keys[...].reshape(512, WIDE)
    for part in range(4):
        at, to = slice(part * 128, part * 128 + 128), slice(part * 8, part * 8 + 8)
        got = dot(choose[at], both)
        packed[to, :, 0:512] = got[:, 0:512].astype(BF16).reshape(8, 16, 512)
        last = jnp.where(lane[at] < 64, got[:, 512:WIDE], bias[at])
        packed[to, :, 512:WIDE] = last.astype(BF16).reshape(8, 16, 128)
        for m in range(part * 8, part * 8 + 8):
            if m == 0:
                pl.when(core == 1)(lambda: a_copy(0).start())
                pl.when(core == 0)(lambda: own_copy.start())
            else:
                a_copy(m).start()

    def resident_keys():
        for i in range(5, len(fetches)):
            fetches[i].wait()
        held = jnp.zeros((16, 64), F32)
        page_ids = iota((16, 64), 0)
        for j in range(8):
            left_over = jnp.clip(res_lengths[...].astype(F32) - 64.0 * j, 0.0, 64.0)
            held = held + jnp.where(tables[j : j + 1, :] == page_ids, left_over, 0.0)
        shift = jnp.where(iota((64, 128), 0) == iota((64, 128), 1) - 64, 1.0, 0.0).astype(BF16)
        held = dot(held.astype(BF16), shift).astype(BF16)
        spread = jnp.where(iota((1024, 16), 0) // 64 == iota((1024, 16), 1), 1.0, 0.0).astype(BF16)
        held = dot(spread, held)
        place = (iota((1024, 128), 0) % 64).astype(F32)
        lane = iota((1024, 128), 1)
        bias = jnp.where((place < held) | (lane < 64), 0.0, -BIG)
        res_keys[0:1024, 512:WIDE] = bias.astype(BF16)
        res_keys[0:1024, 512:LAT] = pool_codes[:, 512:LAT]
        eye = jnp.where(iota((64, 64), 0) == iota((64, 64), 1), 1.0, 0.0).astype(BF16)
        for p in range(16):
            at = slice(p * 64, p * 64 + 64)
            scale_map = dot_t(eye, spread_scales(pool_scales[p]))
            res_keys[at, 0:512] = (pool_codes[at, 0:512].astype(F32) * scale_map).astype(BF16)
        same = iota((128, 128), 0) % 64 == iota((128, 128), 1) - 64
        res_keys[1024:1152, 512:WIDE] = jnp.where(same, 0.0, -BIG).astype(BF16)
        res_keys[1024:1152, 0:LAT] = fresh[...]
        row_of = (iota((1024, 128), 0) // 8) % 64
        wide_q[:, 512:WIDE] = jnp.where(row_of == iota((1024, 128), 1) - 64, 1.0, 0.0).astype(BF16)
        wide_q[:, 0:LAT] = queries[...]

    def resident_block(block):
        rows_at = slice(block * 128, block * 128 + 128)
        query = wide_q[rows_at, :]
        scores = dot_t(query, res_keys[0:1024, :])
        fresh_scores = dot_t(query, res_keys[1024:1152, :])
        if block < 4:
            fresh_scores = jnp.where(iota((128, 128), 1) < 64, fresh_scores, -BIG)
        mixed = softmax_mix(
            scores, fresh_scores, res_keys[0:1024, 0:512], res_keys[1024:1152, 0:512]
        ).astype(F32)
        for tile in range(4):
            lat[tile, rows_at, :] = mixed[:, tile * 128 : tile * 128 + 128]

    def hop(src_x, q, way, device):
        span = GROUPS[q]
        ref = pages_in.at[core, src_x, pl.ds(span[0], span[1] - span[0])]
        return pltpu.make_async_remote_copy(
            src_ref=ref, dst_ref=ref, send_sem=h_send.at[way], recv_sem=h_recv.at[q, way],
            device_id=device, device_id_type=MESH,
        )

    def to_partner(q, from_core):
        span = GROUPS[q]
        ref = pages_in.at[from_core, :, pl.ds(span[0], span[1] - span[0])]
        return pltpu.make_async_remote_copy(
            src_ref=ref, dst_ref=ref, send_sem=p_send, recv_sem=p_recv.at[q],
            device_id=partner, device_id_type=MESH,
        )

    hops = ((far, far_x, 2), (right, left_x, 0), (left, right_x, 1))

    def stage_own(q):
        first, last = GROUPS[q]
        landed = pages_in.at[core, x, pl.ds(first, last - first)]
        pltpu.make_async_copy(landed, landed, a_recv.at[q]).wait()
        for device, _, way in hops:
            hop(x, q, way, device).start()

    def stage_collect(q):
        for device, src_x, way in hops:
            hop(src_x, q, way, device).wait_recv()
        to_partner(q, core).start()

    def stage_done(q):
        to_partner(q, 1 - core).wait_recv()

    slots = 2 * SLOTS

    def meta_first():
        pl.when(jnp.logical_not(to_self))(lambda: meta_copy(0).wait_recv())
        pl.when(to_self)(lambda: meta_own().wait())
        for a in range(1, SLOTS // NX):
            meta_copy(a).wait_recv()
        for i in range(3):
            meta_gather(i).start()

    def meta_second():
        for i in range(3):
            meta_gather(i).wait_recv()
        meta_partner(core).start()

    def owner_of(k):
        dz, dy = slot_offset(k % SLOTS, k // SLOTS)
        return ((z + NZ - dz) % NZ) * NY + (y + 2 * NY - dy) % NY

    def slot_rows_of():
        meta_partner(1 - core).wait_recv()
        k = iota((slots, slots * 8), 0)
        at = ((k // SLOTS) * SLOTS + (k % 4) * (SLOTS // 4) + (k % SLOTS) // 4) * 8
        pick = jnp.where(iota((slots, slots * 8), 1) == at, 1.0, 0.0).astype(BF16)
        present = dot(pick, meta_in[...].reshape(slots * 8, 128).astype(BF16))[:, 0:1]
        eye = iota((slots, slots), 0) == iota((slots, slots), 1)
        present_row = dot(jnp.ones((slots, slots), BF16), jnp.where(eye, present, 0.0).astype(BF16))
        before = owner_of(iota((slots, slots), 1)) < owner_of(iota((slots, slots), 0))
        rank = jnp.sum(jnp.where(before, present_row, 0.0), axis=1, keepdims=True)
        arrivals = jnp.sum(present_row[0:8, :], axis=1, keepdims=True)[0:1, :]
        rank = jnp.where(present > 0.5, rank, -1.0)
        ranks = jnp.broadcast_to(rank, (slots, 128)).astype(BF16)
        widen = jnp.where(iota((512, slots), 0) // 8 == iota((512, slots), 1), 1.0, 0.0)
        rank_col = dot(widen.astype(BF16), ranks)[:, 0:1]
        head_col = (iota((512, 1), 0) % 8).astype(F32)
        goal_col = jnp.where(rank_col > -0.5, rank_col * 8.0 + head_col, -1.0).astype(I32)
        to_slots = jnp.where(goal_col == iota((512, 512), 1), 1.0, 0.0).astype(BF16)
        fresh_pick = jnp.where(rank.astype(I32) == iota((slots, 64), 1), 1.0, 0.0).astype(BF16)
        slot_fresh[:, 512:WIDE] = jnp.zeros((2 * slots, 128), BF16)
        for j in range(2):
            slot_fresh[j * slots : (j + 1) * slots, 0:LAT] = dot(
                fresh_pick, fresh[j * 64 : j * 64 + 64, :]
            ).astype(BF16)
        lane = iota((512, 128), 1)
        mark = jnp.where(lane - 64 == (iota((512, 128), 0) // 8) % 4, 1.0, 0.0)
        for s in range(2):
            got = dot(to_slots, wide_q[s * 512 : s * 512 + 512, :])
            slot_q[:, s, :, 0:512] = got[:, 0:512].astype(BF16).reshape(BLOCKS, 32, 512)
            last = jnp.where(lane < 64, got[:, 512:WIDE], mark).astype(BF16)
            slot_q[:, s, :, 512:WIDE] = last.reshape(BLOCKS, 32, 128)
        n = iota((slots, 128), 1)
        spot = jnp.where(n // 8 * 4 + n % 4 == iota((slots, 128), 0), rank, 0.0)
        rank_row = dot(jnp.ones((8, slots), BF16), spot.astype(BF16))[0:1, :]
        n = iota((128, 128), 1)
        row = iota((128, 128), 0)
        same = (rank_row.astype(I32) == row % 64) & (n // 4 % 2 == row // 64)
        return jnp.where(same, 1.0, 0.0).astype(BF16), arrivals

    def arrived_blocks(*blocks):
        queries_of = [slot_q[block].reshape(64, WIDE) for block in blocks]
        keys_of = []
        for block in blocks:
            at = block % (BLOCKS // 2) * 4
            keys_of.append(pages_in[block // (BLOCKS // 2), :, at : at + 4].reshape(256, WIDE))
        row, lane = iota((64, 2 * slots), 0), iota((64, 2 * slots), 1)
        results = []
        for block, query, page_keys in zip(blocks, queries_of, keys_of):
            scores = dot_t(query, page_keys)
            fresh_scores = dot_t(query, slot_fresh[...])
            slot = block * 4 + (row % 32) // 8
            fresh_ok = (lane % slots == slot) & (lane // slots <= row // 32)
            results.append((scores, jnp.where(fresh_ok, fresh_scores, -BIG)))
        for block, page_keys, (scores, fresh_scores) in zip(blocks, keys_of, results):
            mixed = softmax_mix(scores, fresh_scores, page_keys[:, 0:512], slot_fresh[:, 0:512])
            mixed = mixed.astype(F32)
            for tile in range(4):
                slot_lat[tile, block * 64 : block * 64 + 64, :] = mixed[:, tile * 128 : tile * 128 + 128]

    def project(source, start, count):
        results = []
        for h in range(8):
            at = pl.ds(start * 8 + h, count, stride=8)
            per_head = jnp.concatenate([source[t, at, :].astype(BF16) for t in range(4)], axis=1)
            results.append(dot(per_head, projection[h]).astype(BF16))
        return jnp.concatenate(results, axis=1)

    resident_keys()
    steps = len(GROUPS)
    half = BLOCKS // 2

    def stage_attend(q):
        stage_done(q)
        arrived_blocks(q, q + half)
        if q == half - 2:
            slot_out[0:56, :] = project(slot_lat, 0, 56)
            slot_out[64:120, :] = project(slot_lat, 64, 56)
        if q == half - 1:
            slot_out[56:64, :] = project(slot_lat, 56, 8)
            slot_out[120:128, :] = project(slot_lat, 120, 8)

    for step in range(steps + 2):
        if step < 8:
            resident_block(step)
        if step == 8:
            res_out[...] = project(lat, 0, 128)
        if step < steps:
            stage_own(step)
        if step == 0:
            meta_first()
        if step == 1:
            meta_second()
        if step == 2:
            to_rows, arrivals = slot_rows_of()
        if 1 <= step <= steps:
            stage_collect(step - 1)
        if 2 <= step:
            stage_attend(step - 2)

    moved = dot(to_rows, slot_out[...])
    resident_row = (iota((128, 1), 0) % 64).astype(F32) >= arrivals
    out[...] = jnp.where(resident_row, res_out[...].astype(F32), moved).astype(BF16)

    pl.when(jnp.logical_not(to_self))(lambda: meta_copy(0).wait_send())
    for a in range(1, SLOTS // NX):
        meta_copy(a).wait_send()
    for i in range(3):
        meta_gather(i).wait_send()
    meta_partner(core).wait_send()
    all_own = pages_in.at[core, x]
    for way in range(3):
        pltpu.make_async_copy(all_own, all_own, h_send.at[way]).wait()
    pltpu.make_async_copy(pages_in.at[core], pages_in.at[core], p_send).wait()
    pl.when(core == 1)(lambda: a_copy(0).wait_send())
    pltpu.make_async_copy(packed.at[1:SLOTS], packed.at[1:SLOTS], a_send.at[1]).wait()


def shards(
    prefill_codes, prefill_scales, page_lists, req_lengths, destinations, pool_codes, pool_scales,
    res_tables, res_lengths, queries, new_latents, value_projection,
):
    slots = 2 * SLOTS
    dma = pltpu.SemaphoreType.DMA
    operands = (
        prefill_codes.reshape(256, LAT),
        jnp.transpose(prefill_scales, (1, 2, 0)),
        page_lists.reshape(1, 32),
        req_lengths.reshape(1, 32),
        destinations.reshape(1, 32),
        pool_codes.reshape(1024, LAT),
        jnp.transpose(pool_scales, (0, 2, 1)),
        jnp.transpose(res_tables),
        res_lengths.reshape(1, 64),
        queries.reshape(1024, LAT),
        new_latents.reshape(128, LAT),
        value_projection,
    )
    groups = dma((len(GROUPS),))
    result = pl.pallas_call(
        kernel,
        out_shape=jax.ShapeDtypeStruct((128, 1024), BF16),
        in_specs=[pl.BlockSpec(memory_space=pltpu.HBM)] * 12,
        out_specs=pl.BlockSpec(memory_space=pltpu.VMEM),
        scratch_shapes=[pltpu.VMEM(item.shape, item.dtype) for item in operands]
        + [
            pltpu.VMEM((2, 256, WIDE), BF16),
            pltpu.VMEM((SLOTS, 16, WIDE), BF16),
            pltpu.VMEM((2, NX, SLOTS, 16, WIDE), BF16),
            pltpu.VMEM((1152, WIDE), BF16),
            pltpu.VMEM((1024, WIDE), BF16),
            pltpu.VMEM((BLOCKS, 2, 32, WIDE), BF16),
            pltpu.VMEM((2 * slots, WIDE), BF16),
            pltpu.VMEM((4, BLOCKS * 64, 128), F32),
            pltpu.VMEM((4, 1024, 128), F32),
            pltpu.VMEM((SLOTS, 8, 128), F32),
            pltpu.VMEM((2, NX, SLOTS // NX, 8, 128), F32),
            pltpu.VMEM((128, 1024), BF16),
            pltpu.VMEM((128, 1024), BF16),
            dma((12,)), dma, dma, dma((2,)), groups,
            dma((3,)), dma((len(GROUPS), 3)), dma, groups,
            dma((SLOTS // NX,)), dma((SLOTS // NX,)), dma((4,)), dma((4,)), dma,
        ],
        compiler_params=pltpu.CompilerParams(
            collective_id=0, has_side_effects=True, vmem_limit_bytes=64 * 1024 * 1024
        ),
    )(*operands)
    return result.reshape(2, 64, 1024)


def solution(mesh):
    return jax.shard_map(
        shards,
        mesh=mesh,
        in_specs=(
            P("inst", "head", None),
            P("inst", "head", None),
            P("inst", None),
            P("inst"),
            P("inst"),
            P("inst", None, None),
            P("inst", None, None),
            P("inst", None),
            P("inst"),
            P(None, "inst", "head", None),
            P(None, "inst", None),
            P("head", None, None),
        ),
        out_specs=P(None, "inst", "head"),
        check_vma=False,
    )
```

```python
import functools
import math

import jax
import jax.numpy as jnp
from jax import lax
from jax.experimental import pallas as pl
from jax.experimental.pallas import tpu as pltpu
from jax.sharding import PartitionSpec as P

LATENT_WIDTH = 512
LAT = 576
WIDE = 640
NZ, NY, NX = 16, 4, 4
SLOTS = NZ * NY // 2
BLOCKS = 2 * SLOTS // 4
GROUPS = ((0, 6), (6, 10), (10, 14), (14, 18), (18, 22), (22, 26), (26, 30), (30, 32))
LAST = len(GROUPS) - 1
BIG = 1e30
MESH = pl.DeviceIdType.MESH
softmax_scale = (0.1 * math.log(40.0) + 1.0) ** 2 / math.sqrt(192.0)
F32, BF16, I32 = jnp.float32, jnp.bfloat16, jnp.int32


def iota(shape, axis):
    return lax.broadcasted_iota(I32, shape, axis)


def dot(a, b):
    return lax.dot_general(a, b, (((1,), (0,)), ((), ())), preferred_element_type=F32)


def dot_t(a, b):
    return lax.dot_general(a, b, (((1,), (1,)), ((), ())), preferred_element_type=F32)


def slot_offset(m, core):
    pair = m // 2
    if isinstance(m, int):
        dz = (pair + 1) // 2 if pair % 2 else (NZ - pair // 2) % NZ
    else:
        dz = jnp.where(pair % 2 == 1, (pair + 1) // 2, (NZ - pair // 2) % NZ)
    return dz, 2 * (m % 2) + core


def spread_scales(scales):
    n = scales.shape[1]
    scales = scales.astype(F32)
    spread = [jnp.broadcast_to(scales[j : j + 1, :], (128, n)) for j in range(4)]
    return jnp.concatenate(spread, axis=0).astype(BF16)


def softmax_mix(scores, fresh_scores, values, fresh_values):
    scores = scores * softmax_scale
    fresh_scores = fresh_scores * softmax_scale
    highest = jnp.maximum(
        jnp.max(scores, axis=1, keepdims=True), jnp.max(fresh_scores, axis=1, keepdims=True)
    )
    weights = jnp.exp(scores - highest)
    fresh_weights = jnp.exp(fresh_scores - highest)
    total = jnp.sum(weights, axis=1, keepdims=True) + jnp.sum(fresh_weights, axis=1, keepdims=True)
    mixed = dot(weights.astype(BF16), values) + dot(fresh_weights.astype(BF16), fresh_values)
    return (mixed / total).astype(BF16)


def kernel(
    codes_hbm, scales_hbm, pages_hbm, lengths_hbm, dests_hbm, pool_codes_hbm, pool_scales_hbm,
    tables_hbm, res_lengths_hbm, queries_hbm, fresh_hbm, projection_hbm, out,
    codes, scales, pages, lengths, dests, pool_codes, pool_scales,
    tables, res_lengths, queries, fresh, projection,
    keys, packed, pages_in, res_keys, wide_q, slot_q, slot_fresh, slot_lat, lat,
    meta, meta_in, slot_out, res_out,
    in_sems, key_send, key_recv, a_send, a_recv, h_send, h_recv, p_send, p_recv,
    m_send, m_recv, g_send, g_recv, meta_sem,
):
    sources = (
        codes_hbm, scales_hbm, pages_hbm, lengths_hbm, dests_hbm, pool_codes_hbm, pool_scales_hbm,
        tables_hbm, res_lengths_hbm, queries_hbm, fresh_hbm, projection_hbm,
    )
    places = (
        codes, scales, pages, lengths, dests, pool_codes, pool_scales,
        tables, res_lengths, queries, fresh, projection,
    )
    fetches = [
        pltpu.make_async_copy(src, dst, in_sems.at[i])
        for i, (src, dst) in enumerate(zip(sources, places))
    ]
    for i in range(2):
        fetches[i].start()
    inst, head = lax.axis_index("inst"), lax.axis_index("head")
    z, y = inst // NY, inst % NY
    x, core = head // 2, head % 2
    right_x, left_x, far_x = (x + 1) % NX, (x + NX - 1) % NX, (x + 2) % NX
    right, left, far = (inst, right_x * 2 + core), (inst, left_x * 2 + core), (inst, far_x * 2 + core)
    partner = (inst, x * 2 + 1 - core)

    def target(m):
        dz, dy = slot_offset(m, core)
        return (((z + dz) % NZ) * NY + (y + dy) % NY, head)

    target_of = target

    barrier = pltpu.get_barrier_semaphore()
    for m in reversed(range(SLOTS)):
        if m == 0:
            @pl.when(core == 1)
            def _():
                pl.semaphore_signal(barrier, inc=1, device_id=target(0), device_id_type=MESH)
        else:
            pl.semaphore_signal(barrier, inc=1, device_id=target(m), device_id_type=MESH)

    for device in (partner, right, left, far):
        pl.semaphore_signal(barrier, inc=1, device_id=device, device_id_type=MESH)
    for i in range(2, len(fetches)):
        fetches[i].start()

    own = keys.at[core]
    own[:, 512:WIDE] = jnp.zeros((256, 128), BF16)
    fetches[0].wait()
    fetches[1].wait()
    token_row = iota((256, 32), 0)
    of_page = token_row // 8 == iota((256, 32), 1)
    scale_map = jnp.zeros((256, 512), F32)
    for t in range(8):
        at_token = jnp.where(of_page & (token_row % 8 == t), 1.0, 0.0).astype(BF16)
        scale_map = scale_map + dot_t(at_token, spread_scales(scales[t]))
    own[:, 0:512] = (codes[:, 0:512].astype(F32) * scale_map).astype(BF16)
    own[:, 512:LAT] = codes[:, 512:LAT]
    for i in range(2, 5):
        fetches[i].wait()

    pl.semaphore_wait(barrier, SLOTS + 3 + core)
    key_copy = pltpu.make_async_remote_copy(
        src_ref=own, dst_ref=own, send_sem=key_send, recv_sem=key_recv,
        device_id=partner, device_id_type=MESH,
    )
    key_copy.start()

    rows = SLOTS * 16
    row = iota((rows, 32), 0)
    dz, dy = slot_offset(row // 16, core)
    wanted = ((z + dz) % NZ) * NY + (y + dy) % NY
    hit = dests[...] == wanted
    page = jnp.sum(jnp.where(hit, pages[...].astype(F32) + 1.0, 0.0), axis=1, keepdims=True)
    marks = jnp.broadcast_to(jnp.where(page > 0.5, 1.0, 0.0), (rows, 128))
    meta[...] = marks.reshape(SLOTS, 2, 8, 128)[:, 0]

    def meta_copy(a):
        return pltpu.make_async_remote_copy(
            src_ref=meta.at[4 * a + x], dst_ref=meta_in.at[core, x, a],
            send_sem=m_send.at[a], recv_sem=m_recv.at[a],
            device_id=target_of(4 * a + x), device_id_type=MESH,
        )

    def meta_own():
        return pltpu.make_async_copy(meta.at[0], meta_in.at[core, x, 0], meta_sem)

    to_self = (core == 0) & (x == 0)
    pl.when(jnp.logical_not(to_self))(lambda: meta_copy(0).start())
    pl.when(to_self)(lambda: meta_own().start())
    for a in range(1, SLOTS // NX):
        meta_copy(a).start()

    def meta_gather(i):
        ref = meta_in.at[core, x]
        return pltpu.make_async_remote_copy(
            src_ref=ref, dst_ref=ref, send_sem=g_send.at[i], recv_sem=g_recv.at[i],
            device_id=(right, left, far)[i], device_id_type=MESH,
        )

    def meta_partner(from_core):
        ref = meta_in.at[from_core]
        return pltpu.make_async_remote_copy(
            src_ref=ref, dst_ref=ref, send_sem=g_send.at[3], recv_sem=g_recv.at[3],
            device_id=partner, device_id_type=MESH,
        )

    count = jnp.sum(jnp.where(hit, lengths[...].astype(F32), 0.0), axis=1, keepdims=True)
    slot_row = iota((rows, 1), 0)
    token = slot_row % 16
    column = (token // 8) * 256 + (page.astype(I32) - 1) * 8 + token % 8
    column = jnp.where(page > 0.5, column, -1)
    choose = jnp.where(column == iota((rows, 512), 1), 1.0, 0.0).astype(BF16)
    valid = (x * 16 + token).astype(F32) < count
    lane = iota((rows, 128), 1)
    mine = (lane - 64) == (slot_row // 16) % 4
    bias = jnp.where(lane < 68, jnp.where(mine & valid, 0.0, -BIG), 0.0)

    group_of = [q for q, (first, last) in enumerate(GROUPS) for _ in range(first, last)]

    def a_copy(m):
        return pltpu.make_async_remote_copy(
            src_ref=packed.at[m], dst_ref=pages_in.at[core, x, m],
            send_sem=a_send.at[min(m, 1)], recv_sem=a_recv.at[group_of[m]],
            device_id=target(m), device_id_type=MESH,
        )

    own_copy = pltpu.make_async_copy(packed.at[0], pages_in.at[core, x, 0], a_recv.at[0])
    key_copy.wait()
    both = keys[...].reshape(512, WIDE)
    for part in range(4):
        at, to = slice(part * 128, part * 128 + 128), slice(part * 8, part * 8 + 8)
        got = dot(choose[at], both)
        packed[to, :, 0:512] = got[:, 0:512].astype(BF16).reshape(8, 16, 512)
        last = jnp.where(lane[at] < 64, got[:, 512:WIDE], bias[at])
        packed[to, :, 512:WIDE] = last.astype(BF16).reshape(8, 16, 128)
        for m in range(part * 8, part * 8 + 8):
            if m == 0:
                pl.when(core == 1)(lambda: a_copy(0).start())
                pl.when(core == 0)(lambda: own_copy.start())
            else:
                a_copy(m).start()

    def resident_keys():
        for i in range(5, len(fetches)):
            fetches[i].wait()
        held = jnp.zeros((16, 64), F32)
        page_ids = iota((16, 64), 0)
        for j in range(8):
            left_over = jnp.clip(res_lengths[...].astype(F32) - 64.0 * j, 0.0, 64.0)
            held = held + jnp.where(tables[j : j + 1, :] == page_ids, left_over, 0.0)
        shift = jnp.where(iota((64, 128), 0) == iota((64, 128), 1) - 64, 1.0, 0.0).astype(BF16)
        held = dot(held.astype(BF16), shift).astype(BF16)
        spread = jnp.where(iota((1024, 16), 0) // 64 == iota((1024, 16), 1), 1.0, 0.0).astype(BF16)
        held = dot(spread, held)
        place = (iota((1024, 128), 0) % 64).astype(F32)
        lane = iota((1024, 128), 1)
        bias = jnp.where((place < held) | (lane < 64), 0.0, -BIG)
        res_keys[0:1024, 512:WIDE] = bias.astype(BF16)
        res_keys[0:1024, 512:LAT] = pool_codes[:, 512:LAT]
        eye = jnp.where(iota((64, 64), 0) == iota((64, 64), 1), 1.0, 0.0).astype(BF16)
        for p in range(16):
            at = slice(p * 64, p * 64 + 64)
            scale_map = dot_t(eye, spread_scales(pool_scales[p]))
            res_keys[at, 0:512] = (pool_codes[at, 0:512].astype(F32) * scale_map).astype(BF16)
        same = iota((128, 128), 0) % 64 == iota((128, 128), 1) - 64
        res_keys[1024:1152, 512:WIDE] = jnp.where(same, 0.0, -BIG).astype(BF16)
        res_keys[1024:1152, 0:LAT] = fresh[...]
        row_of = (iota((1024, 128), 0) // 8) % 64
        wide_q[:, 512:WIDE] = jnp.where(row_of == iota((1024, 128), 1) - 64, 1.0, 0.0).astype(BF16)
        wide_q[:, 0:LAT] = queries[...]

    def resident_block(block):
        rows_at = slice(block * 128, block * 128 + 128)
        query = wide_q[rows_at, :]
        scores = dot_t(query, res_keys[0:1024, :])
        fresh_scores = dot_t(query, res_keys[1024:1152, :])
        if block < 4:
            fresh_scores = jnp.where(iota((128, 128), 1) < 64, fresh_scores, -BIG)
        mixed = softmax_mix(
            scores, fresh_scores, res_keys[0:1024, 0:512], res_keys[1024:1152, 0:512]
        ).astype(F32)
        for tile in range(4):
            lat[tile, rows_at, :] = mixed[:, tile * 128 : tile * 128 + 128]

    def hop(src_x, q, way, device):
        span = GROUPS[q]
        ref = pages_in.at[core, src_x, pl.ds(span[0], span[1] - span[0])]
        return pltpu.make_async_remote_copy(
            src_ref=ref, dst_ref=ref, send_sem=h_send.at[way], recv_sem=h_recv.at[q, way],
            device_id=device, device_id_type=MESH,
        )

    def to_partner(q, from_core):
        span = GROUPS[q]
        ref = pages_in.at[from_core, :, pl.ds(span[0], span[1] - span[0])]
        return pltpu.make_async_remote_copy(
            src_ref=ref, dst_ref=ref, send_sem=p_send, recv_sem=p_recv.at[q],
            device_id=partner, device_id_type=MESH,
        )

    def part_to_partner(src_x, q):
        span = GROUPS[q]
        ref = pages_in.at[core, src_x, pl.ds(span[0], span[1] - span[0])]
        return pltpu.make_async_remote_copy(
            src_ref=ref, dst_ref=ref, send_sem=p_send, recv_sem=p_recv.at[q],
            device_id=partner, device_id_type=MESH,
        )

    hops = ((far, far_x, 2), (right, left_x, 0), (left, right_x, 1))

    def stage_own(q):
        first, last = GROUPS[q]
        landed = pages_in.at[core, x, pl.ds(first, last - first)]
        pltpu.make_async_copy(landed, landed, a_recv.at[q]).wait()
        for device, _, way in hops:
            hop(x, q, way, device).start()
        if q == LAST:
            part_to_partner(x, q).start()

    def stage_collect(q):
        for device, src_x, way in reversed(hops):
            hop(src_x, q, way, device).wait_recv()
            if q == LAST:
                part_to_partner(src_x, q).start()
        if q != LAST:
            to_partner(q, core).start()

    def stage_done(q):
        to_partner(q, 1 - core).wait_recv()

    slots = 2 * SLOTS

    def meta_first():
        pl.when(jnp.logical_not(to_self))(lambda: meta_copy(0).wait_recv())
        pl.when(to_self)(lambda: meta_own().wait())
        for a in range(1, SLOTS // NX):
            meta_copy(a).wait_recv()
        for i in range(3):
            meta_gather(i).start()

    def meta_second():
        for i in range(3):
            meta_gather(i).wait_recv()
        meta_partner(core).start()

    def owner_of(k):
        dz, dy = slot_offset(k % SLOTS, k // SLOTS)
        return ((z + NZ - dz) % NZ) * NY + (y + 2 * NY - dy) % NY

    def slot_rows_of():
        meta_partner(1 - core).wait_recv()
        k = iota((slots, slots * 8), 0)
        at = ((k // SLOTS) * SLOTS + (k % 4) * (SLOTS // 4) + (k % SLOTS) // 4) * 8
        pick = jnp.where(iota((slots, slots * 8), 1) == at, 1.0, 0.0).astype(BF16)
        present = dot(pick, meta_in[...].reshape(slots * 8, 128).astype(BF16))[:, 0:1]
        eye = iota((slots, slots), 0) == iota((slots, slots), 1)
        present_row = dot(jnp.ones((slots, slots), BF16), jnp.where(eye, present, 0.0).astype(BF16))
        before = owner_of(iota((slots, slots), 1)) < owner_of(iota((slots, slots), 0))
        rank = jnp.sum(jnp.where(before, present_row, 0.0), axis=1, keepdims=True)
        arrivals = jnp.sum(present_row[0:8, :], axis=1, keepdims=True)[0:1, :]
        rank = jnp.where(present > 0.5, rank, -1.0)
        ranks = jnp.broadcast_to(rank, (slots, 128)).astype(BF16)
        widen = jnp.where(iota((512, slots), 0) // 8 == iota((512, slots), 1), 1.0, 0.0)
        rank_col = dot(widen.astype(BF16), ranks)[:, 0:1]
        head_col = (iota((512, 1), 0) % 8).astype(F32)
        goal_col = jnp.where(rank_col > -0.5, rank_col * 8.0 + head_col, -1.0).astype(I32)
        to_slots = jnp.where(goal_col == iota((512, 512), 1), 1.0, 0.0).astype(BF16)
        fresh_pick = jnp.where(rank.astype(I32) == iota((slots, 64), 1), 1.0, 0.0).astype(BF16)
        slot_fresh[:, 512:WIDE] = jnp.zeros((2 * slots, 128), BF16)
        for j in range(2):
            slot_fresh[j * slots : (j + 1) * slots, 0:LAT] = dot(
                fresh_pick, fresh[j * 64 : j * 64 + 64, :]
            ).astype(BF16)
        lane = iota((512, 128), 1)
        mark = jnp.where(lane - 64 == (iota((512, 128), 0) // 8) % 4, 1.0, 0.0)
        for s in range(2):
            got = dot(to_slots, wide_q[s * 512 : s * 512 + 512, :])
            slot_q[:, s, :, 0:512] = got[:, 0:512].astype(BF16).reshape(BLOCKS, 32, 512)
            last = jnp.where(lane < 64, got[:, 512:WIDE], mark).astype(BF16)
            slot_q[:, s, :, 512:WIDE] = last.reshape(BLOCKS, 32, 128)
        n = iota((slots, 128), 1)
        spot = jnp.where(n // 8 * 4 + n % 4 == iota((slots, 128), 0), rank, 0.0)
        rank_row = dot(jnp.ones((8, slots), BF16), spot.astype(BF16))[0:1, :]
        n = iota((128, 128), 1)
        row = iota((128, 128), 0)
        same = (rank_row.astype(I32) == row % 64) & (n // 4 % 2 == row // 64)
        return jnp.where(same, 1.0, 0.0).astype(BF16), arrivals

    def arrived_blocks(*blocks):
        queries_of = [slot_q[block].reshape(64, WIDE) for block in blocks]
        keys_of = []
        for block in blocks:
            at = block % (BLOCKS // 2) * 4
            keys_of.append(pages_in[block // (BLOCKS // 2), :, at : at + 4].reshape(256, WIDE))
        row, lane = iota((64, 2 * slots), 0), iota((64, 2 * slots), 1)
        results = []
        for block, query, page_keys in zip(blocks, queries_of, keys_of):
            scores = dot_t(query, page_keys)
            fresh_scores = dot_t(query, slot_fresh[...])
            slot = block * 4 + (row % 32) // 8
            fresh_ok = (lane % slots == slot) & (lane // slots <= row // 32)
            results.append((scores, jnp.where(fresh_ok, fresh_scores, -BIG)))
        for block, page_keys, (scores, fresh_scores) in zip(blocks, keys_of, results):
            mixed = softmax_mix(scores, fresh_scores, page_keys[:, 0:512], slot_fresh[:, 0:512])
            mixed = mixed.astype(F32)
            for tile in range(4):
                slot_lat[tile, block * 64 : block * 64 + 64, :] = mixed[:, tile * 128 : tile * 128 + 128]

    def project(source, start, count):
        results = []
        for h in range(8):
            at = pl.ds(start * 8 + h, count, stride=8)
            per_head = jnp.concatenate([source[t, at, :].astype(BF16) for t in range(4)], axis=1)
            results.append(dot(per_head, projection[h]).astype(BF16))
        return jnp.concatenate(results, axis=1)

    resident_keys()
    steps = len(GROUPS)
    half = BLOCKS // 2

    def stage_attend(q):
        stage_done(q)
        arrived_blocks(q, q + half)
        if q == half - 2:
            slot_out[0:56, :] = project(slot_lat, 0, 56)
            slot_out[64:120, :] = project(slot_lat, 64, 56)
        if q == half - 1:
            slot_out[56:64, :] = project(slot_lat, 56, 8)
            slot_out[120:128, :] = project(slot_lat, 120, 8)

    for step in range(steps + 2):
        if step < 8:
            resident_block(step)
        if step == 8:
            res_out[...] = project(lat, 0, 128)
        if step < steps:
            stage_own(step)
        if step == 0:
            meta_first()
        if step == 1:
            meta_second()
        if step == 2:
            to_rows, arrivals = slot_rows_of()
        if 1 <= step <= steps:
            stage_collect(step - 1)
        if 2 <= step:
            stage_attend(step - 2)

    moved = dot(to_rows, slot_out[...])
    resident_row = (iota((128, 1), 0) % 64).astype(F32) >= arrivals
    out[...] = jnp.where(resident_row, res_out[...].astype(F32), moved).astype(BF16)

    pl.when(jnp.logical_not(to_self))(lambda: meta_copy(0).wait_send())
    for a in range(1, SLOTS // NX):
        meta_copy(a).wait_send()
    for i in range(3):
        meta_gather(i).wait_send()
    meta_partner(core).wait_send()
    all_own = pages_in.at[core, x]
    for way in range(3):
        pltpu.make_async_copy(all_own, all_own, h_send.at[way]).wait()
    pltpu.make_async_copy(pages_in.at[core], pages_in.at[core], p_send).wait()
    pl.when(core == 1)(lambda: a_copy(0).wait_send())
    pltpu.make_async_copy(packed.at[1:SLOTS], packed.at[1:SLOTS], a_send.at[1]).wait()


def shards(
    prefill_codes, prefill_scales, page_lists, req_lengths, destinations, pool_codes, pool_scales,
    res_tables, res_lengths, queries, new_latents, value_projection,
):
    slots = 2 * SLOTS
    dma = pltpu.SemaphoreType.DMA
    operands = (
        prefill_codes.reshape(256, LAT),
        jnp.transpose(prefill_scales, (1, 2, 0)),
        page_lists.reshape(1, 32),
        req_lengths.reshape(1, 32),
        destinations.reshape(1, 32),
        pool_codes.reshape(1024, LAT),
        jnp.transpose(pool_scales, (0, 2, 1)),
        jnp.transpose(res_tables),
        res_lengths.reshape(1, 64),
        queries.reshape(1024, LAT),
        new_latents.reshape(128, LAT),
        value_projection,
    )
    groups = dma((len(GROUPS),))
    result = pl.pallas_call(
        kernel,
        out_shape=jax.ShapeDtypeStruct((128, 1024), BF16),
        in_specs=[pl.BlockSpec(memory_space=pltpu.HBM)] * 12,
        out_specs=pl.BlockSpec(memory_space=pltpu.VMEM),
        scratch_shapes=[pltpu.VMEM(item.shape, item.dtype) for item in operands]
        + [
            pltpu.VMEM((2, 256, WIDE), BF16),
            pltpu.VMEM((SLOTS, 16, WIDE), BF16),
            pltpu.VMEM((2, NX, SLOTS, 16, WIDE), BF16),
            pltpu.VMEM((1152, WIDE), BF16),
            pltpu.VMEM((1024, WIDE), BF16),
            pltpu.VMEM((BLOCKS, 2, 32, WIDE), BF16),
            pltpu.VMEM((2 * slots, WIDE), BF16),
            pltpu.VMEM((4, BLOCKS * 64, 128), F32),
            pltpu.VMEM((4, 1024, 128), F32),
            pltpu.VMEM((SLOTS, 8, 128), F32),
            pltpu.VMEM((2, NX, SLOTS // NX, 8, 128), F32),
            pltpu.VMEM((128, 1024), BF16),
            pltpu.VMEM((128, 1024), BF16),
            dma((12,)), dma, dma, dma((2,)), groups,
            dma((3,)), dma((len(GROUPS), 3)), dma, groups,
            dma((SLOTS // NX,)), dma((SLOTS // NX,)), dma((4,)), dma((4,)), dma,
        ],
        compiler_params=pltpu.CompilerParams(
            collective_id=0, has_side_effects=True, vmem_limit_bytes=64 * 1024 * 1024
        ),
    )(*operands)
    return result.reshape(2, 64, 1024)


def solution(mesh):
    return jax.shard_map(
        shards,
        mesh=mesh,
        in_specs=(
            P("inst", "head", None),
            P("inst", "head", None),
            P("inst", None),
            P("inst"),
            P("inst"),
            P("inst", None, None),
            P("inst", None, None),
            P("inst", None),
            P("inst"),
            P(None, "inst", "head", None),
            P(None, "inst", None),
            P("head", None, None),
        ),
        out_specs=P(None, "inst", "head"),
        check_vma=False,
    )
```

```python
import functools
import math

import jax
import jax.numpy as jnp
from jax import lax
from jax.experimental import pallas as pl
from jax.experimental.pallas import tpu as pltpu
from jax.sharding import PartitionSpec as P

LATENT_WIDTH = 512
LAT = 576
WIDE = 640
NZ, NY, NX = 16, 4, 4
SLOTS = NZ * NY // 2
BLOCKS = 2 * SLOTS // 4
GROUPS = ((0, 6), (6, 10), (10, 14), (14, 18), (18, 22), (22, 26), (26, 30), (30, 32))
LAST = len(GROUPS) - 1
BIG = 1e30
MESH = pl.DeviceIdType.MESH
softmax_scale = (0.1 * math.log(40.0) + 1.0) ** 2 / math.sqrt(192.0)
F32, BF16, I32 = jnp.float32, jnp.bfloat16, jnp.int32


def iota(shape, axis):
    return lax.broadcasted_iota(I32, shape, axis)


def dot(a, b):
    return lax.dot_general(a, b, (((1,), (0,)), ((), ())), preferred_element_type=F32)


def dot_t(a, b):
    return lax.dot_general(a, b, (((1,), (1,)), ((), ())), preferred_element_type=F32)


def slot_offset(m, core):
    pair = m // 2
    if isinstance(m, int):
        dz = (pair + 1) // 2 if pair % 2 else (NZ - pair // 2) % NZ
    else:
        dz = jnp.where(pair % 2 == 1, (pair + 1) // 2, (NZ - pair // 2) % NZ)
    return dz, 2 * (m % 2) + core


def spread_scales(scales):
    n = scales.shape[1]
    scales = scales.astype(F32)
    spread = [jnp.broadcast_to(scales[j : j + 1, :], (128, n)) for j in range(4)]
    return jnp.concatenate(spread, axis=0).astype(BF16)


def softmax_mix(scores, fresh_scores, values, fresh_values):
    scores = scores * softmax_scale
    fresh_scores = fresh_scores * softmax_scale
    highest = jnp.maximum(
        jnp.max(scores, axis=1, keepdims=True), jnp.max(fresh_scores, axis=1, keepdims=True)
    )
    weights = jnp.exp(scores - highest)
    fresh_weights = jnp.exp(fresh_scores - highest)
    total = jnp.sum(weights, axis=1, keepdims=True) + jnp.sum(fresh_weights, axis=1, keepdims=True)
    mixed = dot(weights.astype(BF16), values) + dot(fresh_weights.astype(BF16), fresh_values)
    return (mixed / total).astype(BF16)


def kernel(
    codes_hbm, scales_hbm, pages_hbm, lengths_hbm, dests_hbm, pool_codes_hbm, pool_scales_hbm,
    tables_hbm, res_lengths_hbm, queries_hbm, fresh_hbm, projection_hbm, out,
    codes, scales, pages, lengths, dests, pool_codes, pool_scales,
    tables, res_lengths, queries, fresh, projection,
    keys, packed, pages_in, res_keys, wide_q, slot_q, slot_fresh, slot_lat, lat,
    meta, meta_in, slot_out, res_out,
    in_sems, key_send, key_recv, a_send, a_recv, h_send, h_recv, p_send, p_recv,
    m_send, m_recv, g_send, g_recv, meta_sem,
):
    sources = (
        codes_hbm, scales_hbm, pages_hbm, lengths_hbm, dests_hbm, pool_codes_hbm, pool_scales_hbm,
        tables_hbm, res_lengths_hbm, queries_hbm, fresh_hbm, projection_hbm,
    )
    places = (
        codes, scales, pages, lengths, dests, pool_codes, pool_scales,
        tables, res_lengths, queries, fresh, projection,
    )
    fetches = [
        pltpu.make_async_copy(src, dst, in_sems.at[i])
        for i, (src, dst) in enumerate(zip(sources, places))
    ]
    for i in range(2):
        fetches[i].start()
    inst, head = lax.axis_index("inst"), lax.axis_index("head")
    z, y = inst // NY, inst % NY
    x, core = head // 2, head % 2
    right_x, left_x, far_x = (x + 1) % NX, (x + NX - 1) % NX, (x + 2) % NX
    right, left, far = (inst, right_x * 2 + core), (inst, left_x * 2 + core), (inst, far_x * 2 + core)
    partner = (inst, x * 2 + 1 - core)

    def target(m):
        dz, dy = slot_offset(m, core)
        return (((z + dz) % NZ) * NY + (y + dy) % NY, head)

    target_of = target

    barrier = pltpu.get_barrier_semaphore()
    for m in reversed(range(SLOTS)):
        if m == 0:
            @pl.when(core == 1)
            def _():
                pl.semaphore_signal(barrier, inc=1, device_id=target(0), device_id_type=MESH)
        else:
            pl.semaphore_signal(barrier, inc=1, device_id=target(m), device_id_type=MESH)

    for device in (partner, right, left, far):
        pl.semaphore_signal(barrier, inc=1, device_id=device, device_id_type=MESH)
    for i in range(2, len(fetches)):
        fetches[i].start()

    own = keys.at[core]
    own[:, 512:WIDE] = jnp.zeros((256, 128), BF16)
    fetches[0].wait()
    fetches[1].wait()
    token_row = iota((256, 32), 0)
    of_page = token_row // 8 == iota((256, 32), 1)
    scale_map = jnp.zeros((256, 512), F32)
    for t in range(8):
        at_token = jnp.where(of_page & (token_row % 8 == t), 1.0, 0.0).astype(BF16)
        scale_map = scale_map + dot_t(at_token, spread_scales(scales[t]))
    own[:, 0:512] = (codes[:, 0:512].astype(F32) * scale_map).astype(BF16)
    own[:, 512:LAT] = codes[:, 512:LAT]
    for i in range(2, 5):
        fetches[i].wait()

    pl.semaphore_wait(barrier, SLOTS + 3 + core)
    key_copy = pltpu.make_async_remote_copy(
        src_ref=own, dst_ref=own, send_sem=key_send, recv_sem=key_recv,
        device_id=partner, device_id_type=MESH,
    )
    key_copy.start()

    rows = SLOTS * 16
    row = iota((rows, 32), 0)
    dz, dy = slot_offset(row // 16, core)
    wanted = ((z + dz) % NZ) * NY + (y + dy) % NY
    hit = dests[...] == wanted
    page = jnp.sum(jnp.where(hit, pages[...].astype(F32) + 1.0, 0.0), axis=1, keepdims=True)
    marks = jnp.broadcast_to(jnp.where(page > 0.5, 1.0, 0.0), (rows, 128))
    meta[...] = marks.reshape(SLOTS, 2, 8, 128)[:, 0]

    def meta_copy(a):
        return pltpu.make_async_remote_copy(
            src_ref=meta.at[4 * a + x], dst_ref=meta_in.at[core, x, a],
            send_sem=m_send.at[a], recv_sem=m_recv.at[a],
            device_id=target_of(4 * a + x), device_id_type=MESH,
        )

    def meta_own():
        return pltpu.make_async_copy(meta.at[0], meta_in.at[core, x, 0], meta_sem)

    to_self = (core == 0) & (x == 0)
    pl.when(jnp.logical_not(to_self))(lambda: meta_copy(0).start())
    pl.when(to_self)(lambda: meta_own().start())
    for a in range(1, SLOTS // NX):
        meta_copy(a).start()

    def meta_gather(i):
        ref = meta_in.at[core, x]
        return pltpu.make_async_remote_copy(
            src_ref=ref, dst_ref=ref, send_sem=g_send.at[i], recv_sem=g_recv.at[i],
            device_id=(right, left, far)[i], device_id_type=MESH,
        )

    def meta_partner(from_core):
        ref = meta_in.at[from_core]
        return pltpu.make_async_remote_copy(
            src_ref=ref, dst_ref=ref, send_sem=g_send.at[3], recv_sem=g_recv.at[3],
            device_id=partner, device_id_type=MESH,
        )

    count = jnp.sum(jnp.where(hit, lengths[...].astype(F32), 0.0), axis=1, keepdims=True)
    slot_row = iota((rows, 1), 0)
    token = slot_row % 16
    column = (token // 8) * 256 + (page.astype(I32) - 1) * 8 + token % 8
    column = jnp.where(page > 0.5, column, -1)
    choose = jnp.where(column == iota((rows, 512), 1), 1.0, 0.0).astype(BF16)
    valid = (x * 16 + token).astype(F32) < count
    lane = iota((rows, 128), 1)
    mine = (lane - 64) == (slot_row // 16) % 4
    bias = jnp.where(lane < 68, jnp.where(mine & valid, 0.0, -BIG), 0.0)

    group_of = [q for q, (first, last) in enumerate(GROUPS) for _ in range(first, last)]

    def a_copy(m):
        return pltpu.make_async_remote_copy(
            src_ref=packed.at[m], dst_ref=pages_in.at[core, x, m],
            send_sem=a_send.at[min(m, 1)], recv_sem=a_recv.at[group_of[m]],
            device_id=target(m), device_id_type=MESH,
        )

    own_copy = pltpu.make_async_copy(packed.at[0], pages_in.at[core, x, 0], a_recv.at[0])
    key_copy.wait()
    both = keys[...].reshape(512, WIDE)
    for part in range(4):
        at, to = slice(part * 128, part * 128 + 128), slice(part * 8, part * 8 + 8)
        got = dot(choose[at], both)
        packed[to, :, 0:512] = got[:, 0:512].astype(BF16).reshape(8, 16, 512)
        last = jnp.where(lane[at] < 64, got[:, 512:WIDE], bias[at])
        packed[to, :, 512:WIDE] = last.astype(BF16).reshape(8, 16, 128)
        for m in range(part * 8, part * 8 + 8):
            if m == 0:
                pl.when(core == 1)(lambda: a_copy(0).start())
                pl.when(core == 0)(lambda: own_copy.start())
            else:
                a_copy(m).start()

    def resident_keys():
        for i in range(5, len(fetches)):
            fetches[i].wait()
        held = jnp.zeros((16, 64), F32)
        page_ids = iota((16, 64), 0)
        for j in range(8):
            left_over = jnp.clip(res_lengths[...].astype(F32) - 64.0 * j, 0.0, 64.0)
            held = held + jnp.where(tables[j : j + 1, :] == page_ids, left_over, 0.0)
        shift = jnp.where(iota((64, 128), 0) == iota((64, 128), 1) - 64, 1.0, 0.0).astype(BF16)
        held = dot(held.astype(BF16), shift).astype(BF16)
        spread = jnp.where(iota((1024, 16), 0) // 64 == iota((1024, 16), 1), 1.0, 0.0).astype(BF16)
        held = dot(spread, held)
        place = (iota((1024, 128), 0) % 64).astype(F32)
        lane = iota((1024, 128), 1)
        bias = jnp.where((place < held) | (lane < 64), 0.0, -BIG)
        res_keys[0:1024, 512:WIDE] = bias.astype(BF16)
        res_keys[0:1024, 512:LAT] = pool_codes[:, 512:LAT]
        eye = jnp.where(iota((64, 64), 0) == iota((64, 64), 1), 1.0, 0.0).astype(BF16)
        for p in range(16):
            at = slice(p * 64, p * 64 + 64)
            scale_map = dot_t(eye, spread_scales(pool_scales[p]))
            res_keys[at, 0:512] = (pool_codes[at, 0:512].astype(F32) * scale_map).astype(BF16)
        same = iota((128, 128), 0) % 64 == iota((128, 128), 1) - 64
        res_keys[1024:1152, 512:WIDE] = jnp.where(same, 0.0, -BIG).astype(BF16)
        res_keys[1024:1152, 0:LAT] = fresh[...]
        row_of = (iota((1024, 128), 0) // 8) % 64
        wide_q[:, 512:WIDE] = jnp.where(row_of == iota((1024, 128), 1) - 64, 1.0, 0.0).astype(BF16)
        wide_q[:, 0:LAT] = queries[...]

    def resident_block(block):
        rows_at = slice(block * 128, block * 128 + 128)
        query = wide_q[rows_at, :]
        scores = dot_t(query, res_keys[0:1024, :])
        fresh_scores = dot_t(query, res_keys[1024:1152, :])
        if block < 4:
            fresh_scores = jnp.where(iota((128, 128), 1) < 64, fresh_scores, -BIG)
        mixed = softmax_mix(
            scores, fresh_scores, res_keys[0:1024, 0:512], res_keys[1024:1152, 0:512]
        ).astype(F32)
        for tile in range(4):
            lat[tile, rows_at, :] = mixed[:, tile * 128 : tile * 128 + 128]

    def hop(src_x, q, way, device):
        span = GROUPS[q]
        ref = pages_in.at[core, src_x, pl.ds(span[0], span[1] - span[0])]
        return pltpu.make_async_remote_copy(
            src_ref=ref, dst_ref=ref, send_sem=h_send.at[way], recv_sem=h_recv.at[q, way],
            device_id=device, device_id_type=MESH,
        )

    def to_partner(q, from_core):
        span = GROUPS[q]
        ref = pages_in.at[from_core, :, pl.ds(span[0], span[1] - span[0])]
        return pltpu.make_async_remote_copy(
            src_ref=ref, dst_ref=ref, send_sem=p_send, recv_sem=p_recv.at[q],
            device_id=partner, device_id_type=MESH,
        )

    def part_to_partner(src_x, q):
        span = GROUPS[q]
        ref = pages_in.at[core, src_x, pl.ds(span[0], span[1] - span[0])]
        return pltpu.make_async_remote_copy(
            src_ref=ref, dst_ref=ref, send_sem=p_send, recv_sem=p_recv.at[q],
            device_id=partner, device_id_type=MESH,
        )

    hops = ((far, far_x, 2), (right, left_x, 0), (left, right_x, 1))

    def stage_own(q):
        first, last = GROUPS[q]
        landed = pages_in.at[core, x, pl.ds(first, last - first)]
        pltpu.make_async_copy(landed, landed, a_recv.at[q]).wait()
        for device, _, way in hops:
            hop(x, q, way, device).start()
        if q == LAST:
            part_to_partner(x, q).start()

    def stage_collect(q):
        for device, src_x, way in reversed(hops):
            hop(src_x, q, way, device).wait_recv()
            if q == LAST:
                part_to_partner(src_x, q).start()
        if q != LAST:
            to_partner(q, core).start()

    def stage_done(q):
        to_partner(q, 1 - core).wait_recv()

    slots = 2 * SLOTS

    def meta_first():
        pl.when(jnp.logical_not(to_self))(lambda: meta_copy(0).wait_recv())
        pl.when(to_self)(lambda: meta_own().wait())
        for a in range(1, SLOTS // NX):
            meta_copy(a).wait_recv()
        for i in range(3):
            meta_gather(i).start()

    def meta_second():
        for i in range(3):
            meta_gather(i).wait_recv()
        meta_partner(core).start()

    def owner_of(k):
        dz, dy = slot_offset(k % SLOTS, k // SLOTS)
        return ((z + NZ - dz) % NZ) * NY + (y + 2 * NY - dy) % NY

    def slot_rows_of():
        meta_partner(1 - core).wait_recv()
        k = iota((slots, slots * 8), 0)
        at = ((k // SLOTS) * SLOTS + (k % 4) * (SLOTS // 4) + (k % SLOTS) // 4) * 8
        pick = jnp.where(iota((slots, slots * 8), 1) == at, 1.0, 0.0).astype(BF16)
        present = dot(pick, meta_in[...].reshape(slots * 8, 128).astype(BF16))[:, 0:1]
        eye = iota((slots, slots), 0) == iota((slots, slots), 1)
        present_row = dot(jnp.ones((slots, slots), BF16), jnp.where(eye, present, 0.0).astype(BF16))
        before = owner_of(iota((slots, slots), 1)) < owner_of(iota((slots, slots), 0))
        rank = jnp.sum(jnp.where(before, present_row, 0.0), axis=1, keepdims=True)
        arrivals = jnp.sum(present_row[0:8, :], axis=1, keepdims=True)[0:1, :]
        rank = jnp.where(present > 0.5, rank, -1.0)
        ranks = jnp.broadcast_to(rank, (slots, 128)).astype(BF16)
        widen = jnp.where(iota((512, slots), 0) // 8 == iota((512, slots), 1), 1.0, 0.0)
        rank_col = dot(widen.astype(BF16), ranks)[:, 0:1]
        head_col = (iota((512, 1), 0) % 8).astype(F32)
        goal_col = jnp.where(rank_col > -0.5, rank_col * 8.0 + head_col, -1.0).astype(I32)
        to_slots = jnp.where(goal_col == iota((512, 512), 1), 1.0, 0.0).astype(BF16)
        fresh_pick = jnp.where(rank.astype(I32) == iota((slots, 64), 1), 1.0, 0.0).astype(BF16)
        slot_fresh[:, 512:WIDE] = jnp.zeros((2 * slots, 128), BF16)
        for j in range(2):
            slot_fresh[j * slots : (j + 1) * slots, 0:LAT] = dot(
                fresh_pick, fresh[j * 64 : j * 64 + 64, :]
            ).astype(BF16)
        lane = iota((512, 128), 1)
        mark = jnp.where(lane - 64 == (iota((512, 128), 0) // 8) % 4, 1.0, 0.0)
        for s in range(2):
            got = dot(to_slots, wide_q[s * 512 : s * 512 + 512, :])
            slot_q[:, s, :, 0:512] = got[:, 0:512].astype(BF16).reshape(BLOCKS, 32, 512)
            last = jnp.where(lane < 64, got[:, 512:WIDE], mark).astype(BF16)
            slot_q[:, s, :, 512:WIDE] = last.reshape(BLOCKS, 32, 128)
        n = iota((slots, 128), 1)
        spot = jnp.where(n // 8 * 4 + n % 4 == iota((slots, 128), 0), rank, 0.0)
        rank_row = dot(jnp.ones((8, slots), BF16), spot.astype(BF16))[0:1, :]
        n = iota((128, 128), 1)
        row = iota((128, 128), 0)
        same = (rank_row.astype(I32) == row % 64) & (n // 4 % 2 == row // 64)
        return jnp.where(same, 1.0, 0.0).astype(BF16), arrivals

    def arrived_blocks(*blocks):
        queries_of = [slot_q[block].reshape(64, WIDE) for block in blocks]
        keys_of = []
        for block in blocks:
            at = block % (BLOCKS // 2) * 4
            keys_of.append(pages_in[block // (BLOCKS // 2), :, at : at + 4].reshape(256, WIDE))
        row, lane = iota((64, 2 * slots), 0), iota((64, 2 * slots), 1)
        results = []
        for block, query, page_keys in zip(blocks, queries_of, keys_of):
            scores = dot_t(query, page_keys)
            fresh_scores = dot_t(query, slot_fresh[...])
            slot = block * 4 + (row % 32) // 8
            fresh_ok = (lane % slots == slot) & (lane // slots <= row // 32)
            results.append((scores, jnp.where(fresh_ok, fresh_scores, -BIG)))
        for block, page_keys, (scores, fresh_scores) in zip(blocks, keys_of, results):
            mixed = softmax_mix(scores, fresh_scores, page_keys[:, 0:512], slot_fresh[:, 0:512])
            mixed = mixed.astype(F32)
            for tile in range(4):
                slot_lat[tile, block * 64 : block * 64 + 64, :] = mixed[:, tile * 128 : tile * 128 + 128]

    def project(source, start, count):
        results = []
        for h in range(8):
            at = pl.ds(start * 8 + h, count, stride=8)
            per_head = jnp.concatenate([source[t, at, :].astype(BF16) for t in range(4)], axis=1)
            results.append(dot(per_head, projection[h]).astype(BF16))
        return jnp.concatenate(results, axis=1)

    resident_keys()
    steps = len(GROUPS)
    half = BLOCKS // 2

    def stage_attend(q):
        stage_done(q)
        arrived_blocks(q, q + half)
        if q == half - 2:
            slot_out[0:56, :] = project(slot_lat, 0, 56)
            slot_out[64:120, :] = project(slot_lat, 64, 56)
        if q == half - 1:
            slot_out[56:64, :] = project(slot_lat, 56, 8)
            slot_out[120:128, :] = project(slot_lat, 120, 8)

    for step in range(steps + 2):
        if step < 8:
            resident_block(step)
        if step < steps:
            stage_own(step)
        if step == 0:
            meta_first()
        if step == 1:
            meta_second()
        if step == 2:
            to_rows, arrivals = slot_rows_of()
        if 1 <= step <= steps:
            stage_collect(step - 1)
        if step == 8:
            res_out[...] = project(lat, 0, 128)
        if 2 <= step:
            stage_attend(step - 2)

    moved = dot(to_rows, slot_out[...])
    resident_row = (iota((128, 1), 0) % 64).astype(F32) >= arrivals
    out[...] = jnp.where(resident_row, res_out[...].astype(F32), moved).astype(BF16)

    pl.when(jnp.logical_not(to_self))(lambda: meta_copy(0).wait_send())
    for a in range(1, SLOTS // NX):
        meta_copy(a).wait_send()
    for i in range(3):
        meta_gather(i).wait_send()
    meta_partner(core).wait_send()
    all_own = pages_in.at[core, x]
    for way in range(3):
        pltpu.make_async_copy(all_own, all_own, h_send.at[way]).wait()
    pltpu.make_async_copy(pages_in.at[core], pages_in.at[core], p_send).wait()
    pl.when(core == 1)(lambda: a_copy(0).wait_send())
    pltpu.make_async_copy(packed.at[1:SLOTS], packed.at[1:SLOTS], a_send.at[1]).wait()


def shards(
    prefill_codes, prefill_scales, page_lists, req_lengths, destinations, pool_codes, pool_scales,
    res_tables, res_lengths, queries, new_latents, value_projection,
):
    slots = 2 * SLOTS
    dma = pltpu.SemaphoreType.DMA
    operands = (
        prefill_codes.reshape(256, LAT),
        jnp.transpose(prefill_scales, (1, 2, 0)),
        page_lists.reshape(1, 32),
        req_lengths.reshape(1, 32),
        destinations.reshape(1, 32),
        pool_codes.reshape(1024, LAT),
        jnp.transpose(pool_scales, (0, 2, 1)),
        jnp.transpose(res_tables),
        res_lengths.reshape(1, 64),
        queries.reshape(1024, LAT),
        new_latents.reshape(128, LAT),
        value_projection,
    )
    groups = dma((len(GROUPS),))
    result = pl.pallas_call(
        kernel,
        out_shape=jax.ShapeDtypeStruct((128, 1024), BF16),
        in_specs=[pl.BlockSpec(memory_space=pltpu.HBM)] * 12,
        out_specs=pl.BlockSpec(memory_space=pltpu.VMEM),
        scratch_shapes=[pltpu.VMEM(item.shape, item.dtype) for item in operands]
        + [
            pltpu.VMEM((2, 256, WIDE), BF16),
            pltpu.VMEM((SLOTS, 16, WIDE), BF16),
            pltpu.VMEM((2, NX, SLOTS, 16, WIDE), BF16),
            pltpu.VMEM((1152, WIDE), BF16),
            pltpu.VMEM((1024, WIDE), BF16),
            pltpu.VMEM((BLOCKS, 2, 32, WIDE), BF16),
            pltpu.VMEM((2 * slots, WIDE), BF16),
            pltpu.VMEM((4, BLOCKS * 64, 128), F32),
            pltpu.VMEM((4, 1024, 128), F32),
            pltpu.VMEM((SLOTS, 8, 128), F32),
            pltpu.VMEM((2, NX, SLOTS // NX, 8, 128), F32),
            pltpu.VMEM((128, 1024), BF16),
            pltpu.VMEM((128, 1024), BF16),
            dma((12,)), dma, dma, dma((2,)), groups,
            dma((3,)), dma((len(GROUPS), 3)), dma, groups,
            dma((SLOTS // NX,)), dma((SLOTS // NX,)), dma((4,)), dma((4,)), dma,
        ],
        compiler_params=pltpu.CompilerParams(
            collective_id=0, has_side_effects=True, vmem_limit_bytes=64 * 1024 * 1024
        ),
    )(*operands)
    return result.reshape(2, 64, 1024)


def solution(mesh):
    return jax.shard_map(
        shards,
        mesh=mesh,
        in_specs=(
            P("inst", "head", None),
            P("inst", "head", None),
            P("inst", None),
            P("inst"),
            P("inst"),
            P("inst", None, None),
            P("inst", None, None),
            P("inst", None),
            P("inst"),
            P(None, "inst", "head", None),
            P(None, "inst", None),
            P("head", None, None),
        ),
        out_specs=P(None, "inst", "head"),
        check_vma=False,
    )
```
